32 devices in a mesh: chan: 16 (over z, y, x), blk: 2 (over core).
Axes of the slice: x: 2, y: 2, z: 4, core: 2. Of those that a mesh axis runs over, the one named last changes fastest.
Arguments:
- amps: bfloat16 [16, 1024, 1024], P('chan', 'blk'), may hold values from -6 to 6
- six_j: bfloat16 [16, 1024, 1024], P('chan'), may hold values from -0.1875 to 0.1875
- interaction: bfloat16 [16, 1024, 1024], P('chan', 'blk'), may hold values from -0.1875 to 0.1875
- deal: int32 [16], replicated, may hold values from 0 to 15, each once
- pandya_map: int32 [16], replicated, may hold values from 0 to 15, each once
- rows_live: int32 [16], replicated, may hold values from 1 to 1024, 8192 in all
Outputs:
- update: bfloat16 [16, 1024, 1024], P('chan', 'blk')
The draws below stay inside these ranges and needn't reach their ends.
Inputs may be any that keep to these rules, and one draw needn't show every extreme that they name: `deal`: each channel once. `pandya_map`: each channel once. `rows_live`: the counts sum to 16 * 1024 // 2.
All inputs are finite; a program needn't handle non-finite values.
Results may differ from the reference program's by a relative error of at most 0.0057.
Values may be sent and summed in bfloat16 or wider, within the bound.
No kernel may reach another device: no remote copies, remote signals or barrier semaphores. Data moves between devices by JAX's collectives and lax.ppermute only.
A program may use at most 64 MiB of HBM per device.

```python
import math
import jax
import jax.numpy as jnp
import numpy as np
from jax import lax

COLS = 1024
ROWS = 1024
NCH = 16
PW = 64


def block_levels(key, shape, cuts, smallest, largest):
    def one(axis_at, parts):
        heights = jax.random.uniform(jax.random.fold_in(jax.random.fold_in(key, 6), axis_at), (parts,), jnp.float32, smallest / len(cuts), largest / len(cuts))
        return jnp.repeat(jnp.exp(heights), shape[axis_at] // parts).reshape((-1,) + (1,) * (len(shape) - axis_at - 1))

    factor_of = one(*cuts[0])
    for cut in cuts[1:]:
        factor_of = factor_of * one(*cut)
    return factor_of


def length_profile(count, total, bound, lean):
    portions = [(1 << 20) // math.isqrt(grade ** lean) + 1 for grade in range(2, count + 1)]
    rest, counts = total - bound - (count - 1), [1] * (count - 1)
    while rest > 0:
        movable = [i for i in range(count - 1) if counts[i] < bound]
        pool, remaining = sum([portions[i] for i in movable]), rest
        for i in movable:
            more = min(bound - counts[i], max(1, remaining * portions[i] // pool), rest)
            counts[i] = counts[i] + more
            rest = rest - more
    return np.array([bound] + counts)


def ragged(own_key, count, total, most, lean):
    if count == 2:
        one = jax.random.randint(own_key, (), max(1, total - most), min(most, total - 1) + 1)
        return jnp.stack([one, total - one])
    sizes = jnp.asarray(length_profile(count, total, most, lean), jnp.int32)
    twos = (count - 1) // 2
    donor, taker = sizes[1:1 + 2 * twos:2], sizes[2:2 + 2 * twos:2]
    margin = jnp.minimum(donor - 1, most - taker)
    shifted = jax.random.randint(jax.random.fold_in(own_key, 1), (twos,), 0, 1 << 20) % (margin + 1)
    sizes = sizes.at[1:1 + 2 * twos:2].set(donor - shifted).at[2:2 + 2 * twos:2].set(taker + shifted)
    return sizes[jax.random.permutation(jax.random.fold_in(own_key, 2), count)]


def noise(stream_key, extent, scale, limit, shards=(), kind=jnp.bfloat16):
    array = jax.random.normal(stream_key, extent, jnp.float32) * scale
    if len(shards) > 0:
        array = block_levels(stream_key, extent, shards, -0.22, 0.18) * array
    return jnp.clip(array, min=-limit, max=limit).astype(kind)


def setup_inputs(seed: int = 0) -> dict:
    key_of = jax.random.split(jax.random.key(seed), 7)
    amps = noise(key_of[0], (NCH, ROWS, COLS), 1.0, 6.0, ((0, 16), (1, 2)))
    six_j = noise(key_of[1], (NCH, COLS, COLS), COLS ** -0.5, 0.1875, ((0, 16),))
    interaction = noise(key_of[2], (NCH, COLS, COLS), COLS ** -0.5, 0.1875, ((0, 16), (1, 2)))
    deal = jax.random.permutation(key_of[3], NCH).astype(jnp.int32)
    pandya_map = jax.random.permutation(key_of[4], NCH).astype(jnp.int32)
    rows_live = ragged(key_of[5], NCH, NCH * ROWS // 2, ROWS, 2).astype(jnp.int32)
    return dict(amps=amps, six_j=six_j, interaction=interaction, deal=deal, pandya_map=pandya_map, rows_live=rows_live)


def reference(amps, six_j, interaction, deal, pandya_map, rows_live):
    row_ids = jnp.arange(ROWS, dtype=jnp.int32)
    keep = (row_ids[None, :] < rows_live[:, None]).astype(jnp.bfloat16)
    masked = amps * keep[:, :, None]
    grouped = masked.reshape(NCH, ROWS, NCH, PW)
    inv_map = jnp.argsort(pandya_map).astype(jnp.int32)
    inv_deal = jnp.argsort(deal).astype(jnp.int32)

    def one_channel(args):
        which, six_block, inter_block = args
        pieces = grouped[:, :, inv_map[which], :]
        pieces = pieces[inv_deal]
        ph_block = jnp.transpose(pieces, (1, 0, 2)).reshape(ROWS, COLS)
        coupled = jnp.dot(ph_block, six_block, preferred_element_type=jnp.float32).astype(jnp.bfloat16)
        dressed = jnp.dot(coupled, inter_block, preferred_element_type=jnp.float32).astype(jnp.bfloat16)
        back = jnp.dot(dressed, six_block.T, preferred_element_type=jnp.float32).astype(jnp.bfloat16)
        return back

    returned = lax.map(one_channel, (jnp.arange(NCH, dtype=jnp.int32), six_j, interaction))
    returned = returned.reshape(NCH, ROWS, NCH, PW)

    def one_slot(args):
        slot_keep, chan_id = args
        pieces = returned[pandya_map, :, chan_id, :]
        block = jnp.transpose(pieces, (1, 0, 2)).reshape(ROWS, COLS)
        return block * slot_keep[:, None]

    return lax.map(one_slot, (keep, deal))
```

```python
import functools

import jax
import jax.numpy as jnp
from jax import lax
from jax.experimental import pallas as pl
from jax.experimental.pallas import tpu as pltpu
from jax.sharding import PartitionSpec as P

LANES = 128


def live_lanes(first, rows, live):
    ids = first + lax.broadcasted_iota(jnp.int32, (LANES, rows), 1)
    return ids < live


def scatter_kernel(width, map_ref, live_ref, amps_ref, out_ref, tile, turned, in_sem, out_sem):
    rows, cols = amps_ref.shape
    slot = lax.axis_index("chan")
    first = lax.axis_index("blk") * rows
    live = live_ref[slot]
    tiles = cols // LANES
    per_tile = LANES // width
    loads = [
        pltpu.make_async_copy(
            amps_ref.at[:, pl.ds(j * LANES, LANES)], tile.at[j], in_sem.at[j]
        )
        for j in range(tiles)
    ]
    for load in loads:
        load.start()
    keep = live_lanes(first, rows, live)
    stores = []
    for j in range(tiles):
        loads[j].wait()
        turned[pl.ds(j * LANES, LANES), :] = jnp.where(keep, tile[j].T, 0)
        for i in range(per_tile):
            k = j * per_tile + i
            store = pltpu.make_async_copy(
                turned.at[pl.ds(k * width, width), :],
                out_ref.at[pl.ds(pl.multiple_of(map_ref[k] * width, width), width), :],
                out_sem.at[k],
            )
            store.start()
            stores.append(store)
    for store in stores:
        store.wait()


def gather_kernel(width, map_ref, live_ref, back_ref, out_ref, turned, tile, in_sem, out_sem):
    rows, cols = out_ref.shape
    slot = lax.axis_index("chan")
    first = lax.axis_index("blk") * rows
    live = live_ref[slot]
    tiles = cols // LANES
    per_tile = LANES // width
    loads = [
        pltpu.make_async_copy(
            back_ref.at[pl.ds(pl.multiple_of(map_ref[k] * width, width), width), :],
            turned.at[pl.ds(k * width, width), :],
            in_sem.at[k],
        )
        for k in range(cols // width)
    ]
    for load in loads:
        load.start()
    keep = live_lanes(first, rows, live)
    stores = []
    for j in range(tiles):
        for i in range(per_tile):
            loads[j * per_tile + i].wait()
        tile[j] = jnp.where(keep, turned[pl.ds(j * LANES, LANES), :], 0).T
        store = pltpu.make_async_copy(
            tile.at[j], out_ref.at[:, pl.ds(j * LANES, LANES)], out_sem.at[j]
        )
        store.start()
        stores.append(store)
    for store in stores:
        store.wait()


def move(kernel, out_shape, width, pandya_map, rows_live, block):
    cols, rows = out_shape if kernel is scatter_kernel else block.shape
    tile = pltpu.VMEM((cols // LANES, rows, LANES), jnp.bfloat16)
    turned = pltpu.VMEM((cols, rows), jnp.bfloat16)
    tile_sem = pltpu.SemaphoreType.DMA((cols // LANES,))
    group_sem = pltpu.SemaphoreType.DMA((cols // width,))
    if kernel is scatter_kernel:
        scratch = [tile, turned, tile_sem, group_sem]
    else:
        scratch = [turned, tile, group_sem, tile_sem]
    return pl.pallas_call(
        functools.partial(kernel, width),
        out_shape=jax.ShapeDtypeStruct(out_shape, jnp.bfloat16),
        in_specs=[
            pl.BlockSpec(memory_space=pltpu.SMEM),
            pl.BlockSpec(memory_space=pltpu.SMEM),
            pl.BlockSpec(memory_space=pl.ANY),
        ],
        out_specs=pl.BlockSpec(memory_space=pl.ANY),
        scratch_shapes=scratch,
        cost_estimate=pl.CostEstimate(
            flops=0, bytes_accessed=4 * cols * rows, transcendentals=0
        ),
    )(pandya_map, rows_live, block)


def per_device(amps, six_j, interaction, deal, pandya_map, rows_live):
    groups = lax.axis_size("chan")
    _, rows, cols = amps.shape
    width = cols // groups
    whole = lax.all_gather(interaction, "blk", axis=1, tiled=True)[0]
    outgoing = move(scatter_kernel, (cols, rows), width, pandya_map, rows_live, amps[0])
    incoming = lax.all_to_all(
        outgoing.reshape(groups, width, rows), "chan", split_axis=0, concat_axis=0, tiled=True
    )
    six = six_j[0].reshape(groups, width, cols)[deal].reshape(cols, cols)
    right = lax.dot_general(
        whole, six, (((1,), (1,)), ((), ())), preferred_element_type=jnp.float32
    ).astype(jnp.bfloat16)
    both = lax.dot_general(
        right, six, (((0,), (1,)), ((), ())), preferred_element_type=jnp.float32
    ).astype(jnp.bfloat16)
    sending = jnp.dot(
        both, incoming.reshape(cols, rows), preferred_element_type=jnp.float32
    ).astype(jnp.bfloat16)
    arriving = lax.all_to_all(
        sending.reshape(groups, width, rows), "chan", split_axis=0, concat_axis=0, tiled=True
    )
    result = move(
        gather_kernel, (rows, cols), width, pandya_map, rows_live, arriving.reshape(cols, rows)
    )
    return result[None]


def solution(mesh):
    in_specs = (
        P("chan", "blk", None),
        P("chan", None, None),
        P("chan", "blk", None),
        P(),
        P(),
        P(),
    )
    out_specs = P("chan", "blk", None)
    return jax.shard_map(
        per_device, mesh=mesh, in_specs=in_specs, out_specs=out_specs, check_vma=False
    )
```

```python
import functools

import jax
import jax.numpy as jnp
from jax import lax
from jax.experimental import pallas as pl
from jax.experimental.pallas import tpu as pltpu
from jax.sharding import PartitionSpec as P

LANES = 128


def live_lanes(first, rows, live):
    ids = first + lax.broadcasted_iota(jnp.int32, (LANES, rows), 1)
    return ids < live


def scatter_kernel(width, map_ref, live_ref, amps_ref, out_ref, tile, turned, in_sem, out_sem):
    rows, cols = amps_ref.shape
    slot = lax.axis_index("chan")
    first = lax.axis_index("blk") * rows
    live = live_ref[slot]
    tiles = cols // LANES
    per_tile = LANES // width
    loads = [
        pltpu.make_async_copy(
            amps_ref.at[:, pl.ds(j * LANES, LANES)], tile.at[j], in_sem.at[j]
        )
        for j in range(tiles)
    ]
    for load in loads:
        load.start()
    keep = live_lanes(first, rows, live)
    stores = []
    for j in range(tiles):
        loads[j].wait()
        turned[pl.ds(j * LANES, LANES), :] = jnp.where(keep, tile[j].T, 0)
        for i in range(per_tile):
            k = j * per_tile + i
            store = pltpu.make_async_copy(
                turned.at[pl.ds(k * width, width), :],
                out_ref.at[pl.ds(pl.multiple_of(map_ref[k] * width, width), width), :],
                out_sem.at[k],
            )
            store.start()
            stores.append(store)
    for store in stores:
        store.wait()


def gather_kernel(width, map_ref, live_ref, back_ref, out_ref, turned, tile, in_sem, out_sem):
    rows, cols = out_ref.shape
    slot = lax.axis_index("chan")
    first = lax.axis_index("blk") * rows
    live = live_ref[slot]
    tiles = cols // LANES
    per_tile = LANES // width
    loads = [
        pltpu.make_async_copy(
            back_ref.at[pl.ds(pl.multiple_of(map_ref[k] * width, width), width), :],
            turned.at[pl.ds(k * width, width), :],
            in_sem.at[k],
        )
        for k in range(cols // width)
    ]
    for load in loads:
        load.start()
    keep = live_lanes(first, rows, live)
    stores = []
    for j in range(tiles):
        for i in range(per_tile):
            loads[j * per_tile + i].wait()
        tile[j] = jnp.where(keep, turned[pl.ds(j * LANES, LANES), :], 0).T
        store = pltpu.make_async_copy(
            tile.at[j], out_ref.at[:, pl.ds(j * LANES, LANES)], out_sem.at[j]
        )
        store.start()
        stores.append(store)
    for store in stores:
        store.wait()


def move(kernel, out_shape, width, pandya_map, rows_live, block):
    cols, rows = out_shape if kernel is scatter_kernel else block.shape
    tile = pltpu.VMEM((cols // LANES, rows, LANES), jnp.bfloat16)
    turned = pltpu.VMEM((cols, rows), jnp.bfloat16)
    tile_sem = pltpu.SemaphoreType.DMA((cols // LANES,))
    group_sem = pltpu.SemaphoreType.DMA((cols // width,))
    if kernel is scatter_kernel:
        scratch = [tile, turned, tile_sem, group_sem]
    else:
        scratch = [turned, tile, group_sem, tile_sem]
    return pl.pallas_call(
        functools.partial(kernel, width),
        out_shape=jax.ShapeDtypeStruct(out_shape, jnp.bfloat16),
        in_specs=[
            pl.BlockSpec(memory_space=pltpu.SMEM),
            pl.BlockSpec(memory_space=pltpu.SMEM),
            pl.BlockSpec(memory_space=pl.ANY),
        ],
        out_specs=pl.BlockSpec(memory_space=pl.ANY),
        scratch_shapes=scratch,
        cost_estimate=pl.CostEstimate(
            flops=0, bytes_accessed=4 * cols * rows, transcendentals=0
        ),
    )(pandya_map, rows_live, block)


def chain_kernel(width, deal_ref, six_ref, panel_ref, out_ref, six, panel, right, six_sem, panel_sem):
    cols = six.shape[0]
    fetch = [
        pltpu.make_async_copy(
            six_ref.at[pl.ds(pl.multiple_of(deal_ref[s] * width, width), width), :],
            six.at[pl.ds(s * width, width), :],
            six_sem.at[s],
        )
        for s in range(cols // width)
    ]
    fetch_panel = pltpu.make_async_copy(panel_ref, panel, panel_sem)
    fetch_panel.start()
    for copy in fetch:
        copy.start()
    for copy in fetch:
        copy.wait()
    fetch_panel.wait()
    step = min(256, cols)
    across = (((1,), (1,)), ((), ()))

    @pl.loop(0, cols // step)
    def _(i):
        at = pl.ds(pl.multiple_of(i * step, step), step)
        right[at, :] = lax.dot_general(
            six[at, :], panel[...], across, preferred_element_type=jnp.float32
        ).astype(jnp.bfloat16)
        out_ref[at, :] = lax.dot_general(
            right[at, :], six[...], across, preferred_element_type=jnp.float32
        ).astype(jnp.bfloat16)


def chain(width, deal, six, panel):
    cols = six.shape[0]
    square = pltpu.VMEM((cols, cols), jnp.bfloat16)
    return pl.pallas_call(
        functools.partial(chain_kernel, width),
        out_shape=jax.ShapeDtypeStruct((cols, cols), jnp.bfloat16),
        in_specs=[
            pl.BlockSpec(memory_space=pltpu.SMEM),
            pl.BlockSpec(memory_space=pl.ANY),
            pl.BlockSpec(memory_space=pl.ANY),
        ],
        out_specs=pl.BlockSpec(memory_space=pltpu.VMEM),
        scratch_shapes=[
            square,
            square,
            square,
            pltpu.SemaphoreType.DMA((cols // width,)),
            pltpu.SemaphoreType.DMA,
        ],
        compiler_params=pltpu.CompilerParams(vmem_limit_bytes=24 * 1024 * 1024),
        cost_estimate=pl.CostEstimate(
            flops=4 * cols**3, bytes_accessed=6 * cols * cols, transcendentals=0
        ),
    )(deal, six, panel)


def whole_panel(part):
    shares = lax.axis_size("blk")
    me = lax.axis_index("blk")
    rows, cols = part.shape
    whole = jnp.zeros((shares * rows, cols), part.dtype)
    for step in range(shares):
        owner = lax.rem(me + shares - step, shares)
        whole = lax.dynamic_update_slice(whole, part, (owner * rows, 0))
        if step < shares - 1:
            part = lax.ppermute(part, "blk", [(i, (i + 1) % shares) for i in range(shares)])
    return whole


def per_device(amps, six_j, interaction, deal, pandya_map, rows_live):
    groups = lax.axis_size("chan")
    _, rows, cols = amps.shape
    width = cols // groups
    outgoing = move(scatter_kernel, (cols, rows), width, pandya_map, rows_live, amps[0])
    incoming = lax.all_to_all(
        outgoing.reshape(groups, width, rows), "chan", split_axis=0, concat_axis=0, tiled=True
    )
    both = chain(width, deal, six_j[0], whole_panel(interaction[0]))
    sending = jnp.dot(
        both, incoming.reshape(cols, rows), preferred_element_type=jnp.float32
    ).astype(jnp.bfloat16)
    arriving = lax.all_to_all(
        sending.reshape(groups, width, rows), "chan", split_axis=0, concat_axis=0, tiled=True
    )
    result = move(
        gather_kernel, (rows, cols), width, pandya_map, rows_live, arriving.reshape(cols, rows)
    )
    return result[None]


def solution(mesh):
    in_specs = (
        P("chan", "blk", None),
        P("chan", None, None),
        P("chan", "blk", None),
        P(),
        P(),
        P(),
    )
    out_specs = P("chan", "blk", None)
    return jax.shard_map(
        per_device, mesh=mesh, in_specs=in_specs, out_specs=out_specs, check_vma=False
    )
```

```python
import functools

import jax
import jax.numpy as jnp
from jax import lax
from jax.experimental import pallas as pl
from jax.experimental.pallas import tpu as pltpu
from jax.sharding import PartitionSpec as P

LANES = 128


def live_lanes(first, rows, live):
    ids = first + lax.broadcasted_iota(jnp.int32, (LANES, rows), 1)
    return ids < live


def scatter_kernel(
    width, map_ref, live_ref, amps_ref, out_ref, tile, turned, map_in, live_in, sem, out_sem, small
):
    rows, cols = amps_ref.shape
    first = lax.axis_index("blk") * rows
    per_tile = LANES // width
    scalars = [
        pltpu.make_async_copy(map_ref, map_in, small.at[0]),
        pltpu.make_async_copy(live_ref, live_in, small.at[1]),
    ]
    loads = [
        pltpu.make_async_copy(amps_ref.at[:, pl.ds(j * LANES, LANES)], tile.at[j], sem.at[j])
        for j in range(cols // LANES)
    ]
    for copy in scalars + loads:
        copy.start()
    for copy in scalars:
        copy.wait()
    keep = live_lanes(first, rows, live_in[lax.axis_index("chan")])
    stores = []
    for j, load in enumerate(loads):
        load.wait()
        turned[pl.ds(j * LANES, LANES), :] = jnp.where(keep, tile[j].T, 0)
        for k in range(j * per_tile, (j + 1) * per_tile):
            at = pl.multiple_of(map_in[k] * width, width)
            store = pltpu.make_async_copy(
                turned.at[pl.ds(k * width, width), :],
                out_ref.at[pl.ds(at, width), :],
                out_sem.at[k],
            )
            store.start()
            stores.append(store)
    for store in stores:
        store.wait()


def gather_kernel(width, map_ref, live_ref, back_ref, out_ref, tile, sem):
    rows, cols = out_ref.shape
    first = lax.axis_index("blk") * rows
    live = live_ref[lax.axis_index("chan")]
    per_tile = LANES // width
    keep = live_lanes(first, rows, live)
    stores = []
    for j in range(cols // LANES):
        blocks = []
        for i in range(per_tile):
            at = pl.multiple_of(map_ref[j * per_tile + i] * width, width)
            blocks.append(back_ref[pl.ds(at, width), :])
        tile[j] = jnp.where(keep, jnp.concatenate(blocks, axis=0), 0).T
        store = pltpu.make_async_copy(
            tile.at[j], out_ref.at[:, pl.ds(j * LANES, LANES)], sem.at[j]
        )
        store.start()
        stores.append(store)
    for store in stores:
        store.wait()


def scatter(width, pandya_map, rows_live, block):
    rows, cols = block.shape
    count = cols // width
    return pl.pallas_call(
        functools.partial(scatter_kernel, width),
        out_shape=jax.ShapeDtypeStruct((cols, rows), jnp.bfloat16),
        in_specs=[pl.BlockSpec(memory_space=pl.ANY)] * 3,
        out_specs=pl.BlockSpec(memory_space=pl.ANY),
        scratch_shapes=[
            pltpu.VMEM((cols // LANES, rows, LANES), jnp.bfloat16),
            pltpu.VMEM((cols, rows), jnp.bfloat16),
            pltpu.SMEM((count,), jnp.int32),
            pltpu.SMEM((count,), jnp.int32),
            pltpu.SemaphoreType.DMA((cols // LANES,)),
            pltpu.SemaphoreType.DMA((count,)),
            pltpu.SemaphoreType.DMA((2,)),
        ],
        cost_estimate=pl.CostEstimate(
            flops=0, bytes_accessed=4 * cols * rows, transcendentals=0
        ),
    )(pandya_map, rows_live, block)


def gather(width, pandya_map, rows_live, block):
    cols, rows = block.shape
    return pl.pallas_call(
        functools.partial(gather_kernel, width),
        out_shape=jax.ShapeDtypeStruct((rows, cols), jnp.bfloat16),
        in_specs=[
            pl.BlockSpec(memory_space=pltpu.SMEM),
            pl.BlockSpec(memory_space=pltpu.SMEM),
            pl.BlockSpec(memory_space=pltpu.VMEM),
        ],
        out_specs=pl.BlockSpec(memory_space=pl.ANY),
        scratch_shapes=[
            pltpu.VMEM((cols // LANES, rows, LANES), jnp.bfloat16),
            pltpu.SemaphoreType.DMA((cols // LANES,)),
        ],
        compiler_params=pltpu.CompilerParams(vmem_limit_bytes=8 * 1024 * 1024),
        cost_estimate=pl.CostEstimate(
            flops=0, bytes_accessed=4 * cols * rows, transcendentals=0
        ),
    )(pandya_map, rows_live, block)


def chain_kernel(width, deal_ref, six_ref, panel_ref, out_ref, six, panel, right, six_sem, panel_sem):
    cols = six.shape[0]
    fetch = [
        pltpu.make_async_copy(
            six_ref.at[pl.ds(pl.multiple_of(deal_ref[s] * width, width), width), :],
            six.at[pl.ds(s * width, width), :],
            six_sem.at[s],
        )
        for s in range(cols // width)
    ]
    fetch_panel = pltpu.make_async_copy(panel_ref, panel, panel_sem)
    fetch_panel.start()
    for copy in fetch:
        copy.start()
    for copy in fetch:
        copy.wait()
    fetch_panel.wait()
    step = min(256, cols)
    across = (((1,), (1,)), ((), ()))

    @pl.loop(0, cols // step)
    def _(i):
        at = pl.ds(pl.multiple_of(i * step, step), step)
        right[at, :] = lax.dot_general(
            six[at, :], panel[...], across, preferred_element_type=jnp.float32
        ).astype(jnp.bfloat16)
        out_ref[at, :] = lax.dot_general(
            right[at, :], six[...], across, preferred_element_type=jnp.float32
        ).astype(jnp.bfloat16)


def chain(width, deal, six, panel):
    cols = six.shape[0]
    square = pltpu.VMEM((cols, cols), jnp.bfloat16)
    return pl.pallas_call(
        functools.partial(chain_kernel, width),
        out_shape=jax.ShapeDtypeStruct((cols, cols), jnp.bfloat16),
        in_specs=[
            pl.BlockSpec(memory_space=pltpu.SMEM),
            pl.BlockSpec(memory_space=pl.ANY),
            pl.BlockSpec(memory_space=pl.ANY),
        ],
        out_specs=pl.BlockSpec(memory_space=pltpu.VMEM),
        scratch_shapes=[
            square,
            square,
            square,
            pltpu.SemaphoreType.DMA((cols // width,)),
            pltpu.SemaphoreType.DMA,
        ],
        compiler_params=pltpu.CompilerParams(vmem_limit_bytes=24 * 1024 * 1024),
        cost_estimate=pl.CostEstimate(
            flops=4 * cols**3, bytes_accessed=6 * cols * cols, transcendentals=0
        ),
    )(deal, six, panel)


def whole_panel(part):
    shares = lax.axis_size("blk")
    me = lax.axis_index("blk")
    rows, cols = part.shape
    whole = jnp.zeros((shares * rows, cols), part.dtype)
    for step in range(shares):
        owner = lax.rem(me + shares - step, shares)
        whole = lax.dynamic_update_slice(whole, part, (owner * rows, 0))
        if step < shares - 1:
            part = lax.ppermute(part, "blk", [(i, (i + 1) % shares) for i in range(shares)])
    return whole


def per_device(amps, six_j, interaction, deal, pandya_map, rows_live):
    groups = lax.axis_size("chan")
    _, rows, cols = amps.shape
    width = cols // groups
    outgoing = scatter(width, pandya_map, rows_live, amps[0])
    incoming = lax.all_to_all(
        outgoing.reshape(groups, width, rows), "chan", split_axis=0, concat_axis=0, tiled=True
    )
    both = chain(width, deal, six_j[0], whole_panel(interaction[0]))
    sending = jnp.dot(
        both, incoming.reshape(cols, rows), preferred_element_type=jnp.float32
    ).astype(jnp.bfloat16)
    arriving = lax.all_to_all(
        sending.reshape(groups, width, rows), "chan", split_axis=0, concat_axis=0, tiled=True
    )
    result = gather(width, pandya_map, rows_live, arriving.reshape(cols, rows))
    return result[None]


def solution(mesh):
    in_specs = (
        P("chan", "blk", None),
        P("chan", None, None),
        P("chan", "blk", None),
        P(),
        P(),
        P(),
    )
    out_specs = P("chan", "blk", None)
    return jax.shard_map(
        per_device, mesh=mesh, in_specs=in_specs, out_specs=out_specs, check_vma=False
    )
```

```python
import functools

import jax
import jax.numpy as jnp
from jax import lax
from jax.experimental import pallas as pl
from jax.experimental.pallas import tpu as pltpu
from jax.sharding import PartitionSpec as P

LANES = 128
FIRST_TURN = 0


def live_lanes(first, rows, live):
    ids = first + lax.broadcasted_iota(jnp.int32, (LANES, rows), 1)
    return ids < live


def scatter_kernel(
    width, map_ref, live_ref, amps_ref, out_ref, tile, turned, map_in, live_in, sem, out_sem, small
):
    rows, cols = amps_ref.shape
    first = lax.axis_index("blk") * rows
    per_tile = LANES // width
    scalars = [
        pltpu.make_async_copy(map_ref, map_in, small.at[0]),
        pltpu.make_async_copy(live_ref, live_in, small.at[1]),
    ]
    loads = [
        pltpu.make_async_copy(amps_ref.at[:, pl.ds(j * LANES, LANES)], tile.at[j], sem.at[j])
        for j in range(cols // LANES)
    ]
    for copy in scalars + loads:
        copy.start()
    for copy in scalars:
        copy.wait()
    keep = live_lanes(first, rows, live_in[lax.axis_index("chan")])
    stores = []
    for j, load in enumerate(loads):
        load.wait()
        turned[pl.ds(j * LANES, LANES), :] = jnp.where(keep, tile[j].T, 0)
        for k in range(j * per_tile, (j + 1) * per_tile):
            at = pl.multiple_of(map_in[k] * width, width)
            store = pltpu.make_async_copy(
                turned.at[pl.ds(k * width, width), :],
                out_ref.at[pl.ds(at, width), :],
                out_sem.at[k],
            )
            store.start()
            stores.append(store)
    for store in stores:
        store.wait()


def gather_kernel(width, map_ref, live_ref, back_ref, out_ref, tile, sem):
    rows, cols = out_ref.shape
    first = lax.axis_index("blk") * rows
    live = live_ref[lax.axis_index("chan")]
    per_tile = LANES // width
    keep = live_lanes(first, rows, live)
    stores = []
    for j in range(cols // LANES):
        blocks = []
        for i in range(per_tile):
            at = pl.multiple_of(map_ref[j * per_tile + i] * width, width)
            blocks.append(back_ref[pl.ds(at, width), :])
        tile[j] = jnp.where(keep, jnp.concatenate(blocks, axis=0), 0).T
        store = pltpu.make_async_copy(
            tile.at[j], out_ref.at[:, pl.ds(j * LANES, LANES)], sem.at[j]
        )
        store.start()
        stores.append(store)
    for store in stores:
        store.wait()


def scatter(width, pandya_map, rows_live, block):
    rows, cols = block.shape
    count = cols // width
    return pl.pallas_call(
        functools.partial(scatter_kernel, width),
        out_shape=jax.ShapeDtypeStruct((cols, rows), jnp.bfloat16),
        in_specs=[pl.BlockSpec(memory_space=pl.ANY)] * 3,
        out_specs=pl.BlockSpec(memory_space=pl.ANY),
        scratch_shapes=[
            pltpu.VMEM((cols // LANES, rows, LANES), jnp.bfloat16),
            pltpu.VMEM((cols, rows), jnp.bfloat16),
            pltpu.SMEM((count,), jnp.int32),
            pltpu.SMEM((count,), jnp.int32),
            pltpu.SemaphoreType.DMA((cols // LANES,)),
            pltpu.SemaphoreType.DMA((count,)),
            pltpu.SemaphoreType.DMA((2,)),
        ],
        cost_estimate=pl.CostEstimate(
            flops=0, bytes_accessed=4 * cols * rows, transcendentals=0
        ),
    )(pandya_map, rows_live, block)


def gather(width, pandya_map, rows_live, block):
    cols, rows = block.shape
    return pl.pallas_call(
        functools.partial(gather_kernel, width),
        out_shape=jax.ShapeDtypeStruct((rows, cols), jnp.bfloat16),
        in_specs=[
            pl.BlockSpec(memory_space=pltpu.SMEM),
            pl.BlockSpec(memory_space=pltpu.SMEM),
            pl.BlockSpec(memory_space=pltpu.VMEM),
        ],
        out_specs=pl.BlockSpec(memory_space=pl.ANY),
        scratch_shapes=[
            pltpu.VMEM((cols // LANES, rows, LANES), jnp.bfloat16),
            pltpu.SemaphoreType.DMA((cols // LANES,)),
        ],
        compiler_params=pltpu.CompilerParams(vmem_limit_bytes=8 * 1024 * 1024),
        cost_estimate=pl.CostEstimate(
            flops=0, bytes_accessed=4 * cols * rows, transcendentals=0
        ),
    )(pandya_map, rows_live, block)


def chain_kernel(width, turn, shares, *refs):
    deal_ref, six_ref = refs[:2]
    part_refs = refs[2 : 2 + shares]
    out_ref, six, panel, result, deal, deal_sem, six_sem, panel_sem, out_sem = refs[-9:]
    cols = six.shape[0]
    rows = cols // shares
    step = min(256, cols)
    me = lax.axis_index("blk")
    mine = lax.rem(me, 2) == turn

    @pl.when(mine)
    def _():
        fetch_deal = pltpu.make_async_copy(deal_ref, deal, deal_sem)
        fetch_deal.start()
        parts = []
        for i, part_ref in enumerate(part_refs):
            owner = lax.rem(me + shares - i, shares)
            at = pl.ds(pl.multiple_of(owner * rows, rows), rows)
            parts.append(pltpu.make_async_copy(part_ref, panel.at[at, :], panel_sem.at[i]))
        for copy in parts:
            copy.start()
        fetch_deal.wait()
        blocks = [
            pltpu.make_async_copy(
                six_ref.at[pl.ds(pl.multiple_of(deal[s] * width, width), width), :],
                six.at[pl.ds(s * width, width), :],
                six_sem.at[s],
            )
            for s in range(cols // width)
        ]
        for copy in blocks:
            copy.start()
        for copy in blocks + parts:
            copy.wait()
        across = (((1,), (1,)), ((), ()))
        stores = []
        for i in range(cols // step):
            at = pl.ds(i * step, step)
            right = lax.dot_general(
                six[at, :], panel[...], across, preferred_element_type=jnp.float32
            )
            high = right.astype(jnp.bfloat16)
            low = (right - high.astype(jnp.float32)).astype(jnp.bfloat16)
            total = lax.dot_general(high, six[...], across, preferred_element_type=jnp.float32)
            total += lax.dot_general(low, six[...], across, preferred_element_type=jnp.float32)
            result[at, :] = total.astype(jnp.bfloat16)
            store = pltpu.make_async_copy(result.at[at, :], out_ref.at[at, :], out_sem.at[i])
            store.start()
            stores.append(store)
        for store in stores:
            store.wait()


def chain(width, turn, deal, six, parts, before=()):
    cols = six.shape[0]
    shares = len(parts)
    step = min(256, cols)
    any_space = pl.BlockSpec(memory_space=pl.ANY)
    scratch = pltpu.VMEM((cols, cols), jnp.bfloat16)
    return pl.pallas_call(
        functools.partial(chain_kernel, width, turn, shares),
        out_shape=jax.ShapeDtypeStruct((cols, cols), jnp.bfloat16),
        in_specs=[any_space] * (2 + shares + len(before)),
        out_specs=any_space,
        input_output_aliases={2 + shares: 0} if before else {},
        scratch_shapes=[
            scratch,
            scratch,
            scratch,
            pltpu.SMEM((cols // width,), jnp.int32),
            pltpu.SemaphoreType.DMA,
            pltpu.SemaphoreType.DMA((cols // width,)),
            pltpu.SemaphoreType.DMA((shares,)),
            pltpu.SemaphoreType.DMA((cols // step,)),
        ],
        cost_estimate=pl.CostEstimate(
            flops=6 * cols**3, bytes_accessed=6 * cols * cols, transcendentals=0
        ),
    )(deal, six, *parts, *before)


def near_kernel(far_ref, near_ref, sem):
    copy = pltpu.make_async_copy(far_ref, near_ref, sem)
    copy.start()
    copy.wait()


def near(block):
    return pl.pallas_call(
        near_kernel,
        out_shape=jax.ShapeDtypeStruct(block.shape, block.dtype),
        in_specs=[pl.BlockSpec(memory_space=pl.ANY)],
        out_specs=pl.BlockSpec(memory_space=pltpu.VMEM),
        scratch_shapes=[pltpu.SemaphoreType.DMA],
        compiler_params=pltpu.CompilerParams(vmem_limit_bytes=4 * 1024 * 1024),
        cost_estimate=pl.CostEstimate(
            flops=0, bytes_accessed=4 * block.size, transcendentals=0
        ),
    )(block)


def panel_parts(part):
    shares = lax.axis_size("blk")
    parts = [part]
    for _ in range(shares - 1):
        part = lax.ppermute(part, "blk", [(i, (i + 1) % shares) for i in range(shares)])
        parts.append(part)
    return parts


def per_device(amps, six_j, interaction, deal, pandya_map, rows_live):
    groups = lax.axis_size("chan")
    _, rows, cols = amps.shape
    width = cols // groups
    parts = panel_parts(interaction[0])
    outgoing = scatter(width, pandya_map, rows_live, amps[0])
    both = chain(width, FIRST_TURN, deal, six_j[0], parts)
    outgoing, both = lax.optimization_barrier((outgoing, both))
    incoming = lax.all_to_all(
        outgoing.reshape(groups, width, rows), "chan", split_axis=0, concat_axis=0, tiled=True
    )
    both = chain(width, 1 - FIRST_TURN, deal, six_j[0], parts, (both,))
    both = near(both)
    sending = jnp.dot(
        both, incoming.reshape(cols, rows), preferred_element_type=jnp.float32
    ).astype(jnp.bfloat16)
    arriving = lax.all_to_all(
        sending.reshape(groups, width, rows), "chan", split_axis=0, concat_axis=0, tiled=True
    )
    result = gather(width, pandya_map, rows_live, arriving.reshape(cols, rows))
    return result[None]


def solution(mesh):
    in_specs = (
        P("chan", "blk", None),
        P("chan", None, None),
        P("chan", "blk", None),
        P(),
        P(),
        P(),
    )
    out_specs = P("chan", "blk", None)
    return jax.shard_map(
        per_device, mesh=mesh, in_specs=in_specs, out_specs=out_specs, check_vma=False
    )
```

```python
import functools

import jax
import jax.numpy as jnp
from jax import lax
from jax.experimental import pallas as pl
from jax.experimental.pallas import tpu as pltpu
from jax.sharding import PartitionSpec as P

LANES = 128
AHEAD = 0
TERMS = 3


def live_lanes(first, rows, live):
    ids = first + lax.broadcasted_iota(jnp.int32, (LANES, rows), 1)
    return ids < live


def scatter_kernel(
    width, map_ref, live_ref, amps_ref, out_ref, tile, turned, map_in, live_in, sem, out_sem, small
):
    rows, cols = amps_ref.shape
    first = lax.axis_index("blk") * rows
    per_tile = LANES // width
    scalars = [
        pltpu.make_async_copy(map_ref, map_in, small.at[0]),
        pltpu.make_async_copy(live_ref, live_in, small.at[1]),
    ]
    loads = [
        pltpu.make_async_copy(amps_ref.at[:, pl.ds(j * LANES, LANES)], tile.at[j], sem.at[j])
        for j in range(cols // LANES)
    ]
    for copy in scalars + loads:
        copy.start()
    for copy in scalars:
        copy.wait()
    keep = live_lanes(first, rows, live_in[lax.axis_index("chan")])
    stores = []
    for j, load in enumerate(loads):
        load.wait()
        turned[pl.ds(j * LANES, LANES), :] = jnp.where(keep, tile[j].T, 0)
        for k in range(j * per_tile, (j + 1) * per_tile):
            at = pl.multiple_of(map_in[k] * width, width)
            store = pltpu.make_async_copy(
                turned.at[pl.ds(k * width, width), :],
                out_ref.at[pl.ds(at, width), :],
                out_sem.at[k],
            )
            store.start()
            stores.append(store)
    for store in stores:
        store.wait()


def gather_kernel(width, map_ref, live_ref, back_ref, out_ref, tile, sem):
    rows, cols = out_ref.shape
    first = lax.axis_index("blk") * rows
    live = live_ref[lax.axis_index("chan")]
    per_tile = LANES // width
    keep = live_lanes(first, rows, live)
    stores = []
    for j in range(cols // LANES):
        blocks = []
        for i in range(per_tile):
            at = pl.multiple_of(map_ref[j * per_tile + i] * width, width)
            blocks.append(back_ref[pl.ds(at, width), :])
        tile[j] = jnp.where(keep, jnp.concatenate(blocks, axis=0), 0).T
        store = pltpu.make_async_copy(
            tile.at[j], out_ref.at[:, pl.ds(j * LANES, LANES)], sem.at[j]
        )
        store.start()
        stores.append(store)
    for store in stores:
        store.wait()


def scatter(width, pandya_map, rows_live, block):
    rows, cols = block.shape
    count = cols // width
    return pl.pallas_call(
        functools.partial(scatter_kernel, width),
        out_shape=jax.ShapeDtypeStruct((cols, rows), jnp.bfloat16),
        in_specs=[pl.BlockSpec(memory_space=pl.ANY)] * 3,
        out_specs=pl.BlockSpec(memory_space=pl.ANY),
        scratch_shapes=[
            pltpu.VMEM((cols // LANES, rows, LANES), jnp.bfloat16),
            pltpu.VMEM((cols, rows), jnp.bfloat16),
            pltpu.SMEM((count,), jnp.int32),
            pltpu.SMEM((count,), jnp.int32),
            pltpu.SemaphoreType.DMA((cols // LANES,)),
            pltpu.SemaphoreType.DMA((count,)),
            pltpu.SemaphoreType.DMA((2,)),
        ],
        cost_estimate=pl.CostEstimate(
            flops=0, bytes_accessed=4 * cols * rows, transcendentals=0
        ),
    )(pandya_map, rows_live, block)


def gather(width, pandya_map, rows_live, block):
    cols, rows = block.shape
    return pl.pallas_call(
        functools.partial(gather_kernel, width),
        out_shape=jax.ShapeDtypeStruct((rows, cols), jnp.bfloat16),
        in_specs=[
            pl.BlockSpec(memory_space=pltpu.SMEM),
            pl.BlockSpec(memory_space=pltpu.SMEM),
            pl.BlockSpec(memory_space=pltpu.VMEM),
        ],
        out_specs=pl.BlockSpec(memory_space=pl.ANY),
        scratch_shapes=[
            pltpu.VMEM((cols // LANES, rows, LANES), jnp.bfloat16),
            pltpu.SemaphoreType.DMA((cols // LANES,)),
        ],
        compiler_params=pltpu.CompilerParams(vmem_limit_bytes=8 * 1024 * 1024),
        cost_estimate=pl.CostEstimate(
            flops=0, bytes_accessed=4 * cols * rows, transcendentals=0
        ),
    )(pandya_map, rows_live, block)


def add_part(six, at, part, across_at, total, terms):
    across = (((1,), (1,)), ((), ()))
    rest = lax.dot_general(six[at, :], part, across, preferred_element_type=jnp.float32)
    for _ in range(terms):
        term = rest.astype(jnp.bfloat16)
        rest = rest - term.astype(jnp.float32)
        share = lax.dot_general(
            term, six[:, across_at], across, preferred_element_type=jnp.float32
        )
        total = share if total is None else total + share
    return total


def fetch_six(width, deal_ref, six_ref, deal, six, deal_sem, six_sem):
    fetch_deal = pltpu.make_async_copy(deal_ref, deal, deal_sem)
    fetch_deal.start()
    fetch_deal.wait()
    blocks = [
        pltpu.make_async_copy(
            six_ref.at[pl.ds(pl.multiple_of(deal[s] * width, width), width), :],
            six.at[pl.ds(s * width, width), :],
            six_sem.at[s],
        )
        for s in range(six.shape[0] // width)
    ]
    for copy in blocks:
        copy.start()
    return blocks


def owner_range(i, shares, rows):
    owner = lax.rem(lax.axis_index("blk") + shares - i, shares)
    return pl.ds(pl.multiple_of(owner * rows, rows), rows)


def ahead_tiles(cols):
    step = min(256, cols)
    starts = [0, step // 2] + list(range(step, cols, step))
    return [(a, b - a) for a, b in zip(starts, starts[1:] + [cols])]


def ahead_kernel(
    width, shares, deal_ref, six_ref, part_ref, sum_ref, six, part, total, deal, deal_sem, six_sem, part_sem, out_sem
):
    cols = six.shape[0]
    tiles = ahead_tiles(cols)

    @pl.when(lax.rem(lax.axis_index("blk"), 2) == AHEAD)
    def _():
        fetch_part = pltpu.make_async_copy(part_ref, part, part_sem)
        fetch_part.start()
        for copy in fetch_six(width, deal_ref, six_ref, deal, six, deal_sem, six_sem):
            copy.wait()
        fetch_part.wait()
        stores = []
        for i, (start, size) in enumerate(tiles):
            at = pl.ds(start, size)
            total[at, :] = add_part(
                six, at, part[...], owner_range(0, shares, part.shape[0]), None, TERMS
            )
            store = pltpu.make_async_copy(total.at[at, :], sum_ref.at[at, :], out_sem.at[i])
            store.start()
            stores.append(store)
        for store in stores:
            store.wait()


def ahead(width, shares, deal, six, part):
    cols = six.shape[0]
    any_space = pl.BlockSpec(memory_space=pl.ANY)
    return pl.pallas_call(
        functools.partial(ahead_kernel, width, shares),
        out_shape=jax.ShapeDtypeStruct((cols, cols), jnp.float32),
        in_specs=[any_space] * 3,
        out_specs=any_space,
        scratch_shapes=[
            pltpu.VMEM((cols, cols), jnp.bfloat16),
            pltpu.VMEM(part.shape, jnp.bfloat16),
            pltpu.VMEM((cols, cols), jnp.float32),
            pltpu.SMEM((cols // width,), jnp.int32),
            pltpu.SemaphoreType.DMA,
            pltpu.SemaphoreType.DMA((cols // width,)),
            pltpu.SemaphoreType.DMA,
            pltpu.SemaphoreType.DMA((len(ahead_tiles(cols)),)),
        ],
        cost_estimate=pl.CostEstimate(
            flops=2 * cols**3, bytes_accessed=8 * cols * cols, transcendentals=0
        ),
    )(deal, six, part)


def chain_kernel(width, shares, *refs):
    deal_ref, six_ref = refs[:2]
    part_refs = refs[2 : 2 + shares]
    sum_ref, out_ref, six, part, total, result, deal, deal_sem, six_sem, part_sem, sum_sem, out_sem = (
        refs[2 + shares :]
    )
    cols = six.shape[0]
    step = min(256, cols)
    rows = cols // shares
    was_ahead = lax.rem(lax.axis_index("blk"), 2) == AHEAD

    def form(first):
        if first:
            fetch_sum = pltpu.make_async_copy(sum_ref, total, sum_sem)
            fetch_sum.start()
        parts = [
            pltpu.make_async_copy(part_refs[i], part.at[i], part_sem.at[i])
            for i in range(first, shares)
        ]
        for copy in parts:
            copy.start()
        blocks = fetch_six(width, deal_ref, six_ref, deal, six, deal_sem, six_sem)
        for copy in blocks + parts:
            copy.wait()
        if first:
            fetch_sum.wait()
        stores = []
        for i in range(cols // step):
            at = pl.ds(i * step, step)
            value = total[at, :] if first else None
            for p in range(first, shares):
                value = add_part(six, at, part[p], owner_range(p, shares, rows), value, TERMS)
            result[at, :] = value.astype(jnp.bfloat16)
            store = pltpu.make_async_copy(result.at[at, :], out_ref.at[at, :], out_sem.at[i])
            store.start()
            stores.append(store)
        for store in stores:
            store.wait()

    @pl.when(was_ahead)
    def _():
        form(1)

    @pl.when(jnp.logical_not(was_ahead))
    def _():
        form(0)


def chain(width, deal, six, parts, formed):
    cols = six.shape[0]
    shares = len(parts)
    any_space = pl.BlockSpec(memory_space=pl.ANY)
    return pl.pallas_call(
        functools.partial(chain_kernel, width, shares),
        out_shape=jax.ShapeDtypeStruct((cols, cols), jnp.bfloat16),
        in_specs=[any_space] * (3 + shares),
        out_specs=any_space,
        scratch_shapes=[
            pltpu.VMEM((cols, cols), jnp.bfloat16),
            pltpu.VMEM((shares,) + parts[0].shape, jnp.bfloat16),
            pltpu.VMEM((cols, cols), jnp.float32),
            pltpu.VMEM((cols, cols), jnp.bfloat16),
            pltpu.SMEM((cols // width,), jnp.int32),
            pltpu.SemaphoreType.DMA,
            pltpu.SemaphoreType.DMA((cols // width,)),
            pltpu.SemaphoreType.DMA((shares,)),
            pltpu.SemaphoreType.DMA,
            pltpu.SemaphoreType.DMA((cols // min(256, cols),)),
        ],
        cost_estimate=pl.CostEstimate(
            flops=6 * cols**3, bytes_accessed=6 * cols * cols, transcendentals=0
        ),
    )(deal, six, *parts, formed)


def near_kernel(far_ref, near_ref, sem):
    copy = pltpu.make_async_copy(far_ref, near_ref, sem)
    copy.start()
    copy.wait()


def near(block):
    return pl.pallas_call(
        near_kernel,
        out_shape=jax.ShapeDtypeStruct(block.shape, block.dtype),
        in_specs=[pl.BlockSpec(memory_space=pl.ANY)],
        out_specs=pl.BlockSpec(memory_space=pltpu.VMEM),
        scratch_shapes=[pltpu.SemaphoreType.DMA],
        compiler_params=pltpu.CompilerParams(vmem_limit_bytes=4 * 1024 * 1024),
        cost_estimate=pl.CostEstimate(
            flops=0, bytes_accessed=4 * block.size, transcendentals=0
        ),
    )(block)


def panel_parts(part):
    shares = lax.axis_size("blk")
    parts = [part]
    for _ in range(shares - 1):
        part = lax.ppermute(part, "blk", [(i, (i + 1) % shares) for i in range(shares)])
        parts.append(part)
    return parts


def per_device(amps, six_j, interaction, deal, pandya_map, rows_live):
    groups = lax.axis_size("chan")
    _, rows, cols = amps.shape
    width = cols // groups
    parts = panel_parts(interaction[0])
    outgoing = scatter(width, pandya_map, rows_live, amps[0])
    formed = ahead(width, len(parts), deal, six_j[0], parts[0])
    outgoing, formed, *parts = lax.optimization_barrier((outgoing, formed, *parts))
    incoming = lax.all_to_all(
        outgoing.reshape(groups, width, rows), "chan", split_axis=0, concat_axis=0, tiled=True
    )
    both = chain(width, deal, six_j[0], parts, formed)
    both = near(both)
    sending = jnp.dot(
        both, incoming.reshape(cols, rows), preferred_element_type=jnp.float32
    ).astype(jnp.bfloat16)
    arriving = lax.all_to_all(
        sending.reshape(groups, width, rows), "chan", split_axis=0, concat_axis=0, tiled=True
    )
    result = gather(width, pandya_map, rows_live, arriving.reshape(cols, rows))
    return result[None]


def solution(mesh):
    in_specs = (
        P("chan", "blk", None),
        P("chan", None, None),
        P("chan", "blk", None),
        P(),
        P(),
        P(),
    )
    out_specs = P("chan", "blk", None)
    return jax.shard_map(
        per_device, mesh=mesh, in_specs=in_specs, out_specs=out_specs, check_vma=False
    )
```

```python
import functools

import jax
import jax.numpy as jnp
from jax import lax
from jax.experimental import pallas as pl
from jax.experimental.pallas import tpu as pltpu
from jax.sharding import PartitionSpec as P

LANES = 128
AHEAD = 0
RANK_BITS = (3, 2, 0, 1)
TERMS = 3


def rank_bits(groups):
    return RANK_BITS if groups == 1 << len(RANK_BITS) else range((groups - 1).bit_length())


def ranks(groups):
    if groups & (groups - 1):
        return list(range(groups))
    bits = rank_bits(groups)
    return [sum(((r >> i) & 1) << bit for i, bit in enumerate(bits)) for r in range(groups)]


def rank_of(place, groups):
    if groups & (groups - 1):
        return place
    bits = rank_bits(groups)
    return sum(((place >> bit) & 1) << i for i, bit in enumerate(bits))


def live_lanes(first, rows, live):
    ids = first + lax.broadcasted_iota(jnp.int32, (LANES, rows), 1)
    return ids < live


def scatter_kernel(
    width, map_ref, live_ref, amps_ref, out_ref, tile, turned, map_in, live_in, sem, out_sem, small
):
    rows, cols = amps_ref.shape
    first = lax.axis_index("blk") * rows
    per_tile = LANES // width
    scalars = [
        pltpu.make_async_copy(map_ref, map_in, small.at[0]),
        pltpu.make_async_copy(live_ref, live_in, small.at[1]),
    ]
    loads = [
        pltpu.make_async_copy(amps_ref.at[:, pl.ds(j * LANES, LANES)], tile.at[j], sem.at[j])
        for j in range(cols // LANES)
    ]
    for copy in scalars + loads:
        copy.start()
    for copy in scalars:
        copy.wait()
    keep = live_lanes(first, rows, live_in[lax.axis_index("chan")])
    stores = []
    for j, load in enumerate(loads):
        load.wait()
        turned[pl.ds(j * LANES, LANES), :] = jnp.where(keep, tile[j].T, 0)
        for k in range(j * per_tile, (j + 1) * per_tile):
            at = pl.multiple_of(rank_of(map_in[k], cols // width) * width, width)
            store = pltpu.make_async_copy(
                turned.at[pl.ds(k * width, width), :],
                out_ref.at[pl.ds(at, width), :],
                out_sem.at[k],
            )
            store.start()
            stores.append(store)
    for store in stores:
        store.wait()


def gather_kernel(width, map_ref, live_ref, back_ref, out_ref, tile, sem):
    rows, cols = out_ref.shape
    first = lax.axis_index("blk") * rows
    live = live_ref[lax.axis_index("chan")]
    per_tile = LANES // width
    keep = live_lanes(first, rows, live)
    stores = []
    for j in range(cols // LANES):
        blocks = []
        for i in range(per_tile):
            rank = rank_of(map_ref[j * per_tile + i], cols // width)
            at = pl.multiple_of(rank * width, width)
            blocks.append(back_ref[pl.ds(at, width), :])
        tile[j] = jnp.where(keep, jnp.concatenate(blocks, axis=0), 0).T
        store = pltpu.make_async_copy(
            tile.at[j], out_ref.at[:, pl.ds(j * LANES, LANES)], sem.at[j]
        )
        store.start()
        stores.append(store)
    for store in stores:
        store.wait()


def scatter(width, pandya_map, rows_live, block):
    rows, cols = block.shape
    count = cols // width
    return pl.pallas_call(
        functools.partial(scatter_kernel, width),
        out_shape=jax.ShapeDtypeStruct((cols, rows), jnp.bfloat16),
        in_specs=[pl.BlockSpec(memory_space=pl.ANY)] * 3,
        out_specs=pl.BlockSpec(memory_space=pl.ANY),
        scratch_shapes=[
            pltpu.VMEM((cols // LANES, rows, LANES), jnp.bfloat16),
            pltpu.VMEM((cols, rows), jnp.bfloat16),
            pltpu.SMEM((count,), jnp.int32),
            pltpu.SMEM((count,), jnp.int32),
            pltpu.SemaphoreType.DMA((cols // LANES,)),
            pltpu.SemaphoreType.DMA((count,)),
            pltpu.SemaphoreType.DMA((2,)),
        ],
        cost_estimate=pl.CostEstimate(
            flops=0, bytes_accessed=4 * cols * rows, transcendentals=0
        ),
    )(pandya_map, rows_live, block)


def gather(width, pandya_map, rows_live, block):
    cols, rows = block.shape
    return pl.pallas_call(
        functools.partial(gather_kernel, width),
        out_shape=jax.ShapeDtypeStruct((rows, cols), jnp.bfloat16),
        in_specs=[
            pl.BlockSpec(memory_space=pltpu.SMEM),
            pl.BlockSpec(memory_space=pltpu.SMEM),
            pl.BlockSpec(memory_space=pltpu.VMEM),
        ],
        out_specs=pl.BlockSpec(memory_space=pl.ANY),
        scratch_shapes=[
            pltpu.VMEM((cols // LANES, rows, LANES), jnp.bfloat16),
            pltpu.SemaphoreType.DMA((cols // LANES,)),
        ],
        compiler_params=pltpu.CompilerParams(vmem_limit_bytes=8 * 1024 * 1024),
        cost_estimate=pl.CostEstimate(
            flops=0, bytes_accessed=4 * cols * rows, transcendentals=0
        ),
    )(pandya_map, rows_live, block)


def add_part(six, at, part, across_at, total, terms):
    across = (((1,), (1,)), ((), ()))
    rest = lax.dot_general(six[at, :], part, across, preferred_element_type=jnp.float32)
    for _ in range(terms):
        term = rest.astype(jnp.bfloat16)
        rest = rest - term.astype(jnp.float32)
        share = lax.dot_general(
            term, six[:, across_at], across, preferred_element_type=jnp.float32
        )
        total = share if total is None else total + share
    return total


def fetch_six(width, deal_ref, six_ref, deal, six, deal_sem, six_sem):
    fetch_deal = pltpu.make_async_copy(deal_ref, deal, deal_sem)
    fetch_deal.start()
    fetch_deal.wait()
    blocks = [
        pltpu.make_async_copy(
            six_ref.at[pl.ds(pl.multiple_of(deal[s] * width, width), width), :],
            six.at[pl.ds(r * width, width), :],
            six_sem.at[r],
        )
        for r, s in enumerate(ranks(six.shape[0] // width))
    ]
    for copy in blocks:
        copy.start()
    return blocks


def owner_range(i, shares, rows):
    owner = lax.rem(lax.axis_index("blk") + shares - i, shares)
    return pl.ds(pl.multiple_of(owner * rows, rows), rows)


def ahead_tiles(cols):
    step = min(256, cols)
    starts = [0, step // 2] + list(range(step, cols, step))
    return [(a, b - a) for a, b in zip(starts, starts[1:] + [cols])]


def ahead_kernel(
    width, shares, deal_ref, six_ref, part_ref, sum_ref, six, part, total, deal, deal_sem, six_sem, part_sem, out_sem
):
    cols = six.shape[0]
    tiles = ahead_tiles(cols)

    @pl.when(lax.rem(lax.axis_index("blk"), 2) == AHEAD)
    def _():
        fetch_part = pltpu.make_async_copy(part_ref, part, part_sem)
        fetch_part.start()
        for copy in fetch_six(width, deal_ref, six_ref, deal, six, deal_sem, six_sem):
            copy.wait()
        fetch_part.wait()
        stores = []
        for i, (start, size) in enumerate(tiles):
            at = pl.ds(start, size)
            total[at, :] = add_part(
                six, at, part[...], owner_range(0, shares, part.shape[0]), None, TERMS
            )
            store = pltpu.make_async_copy(total.at[at, :], sum_ref.at[at, :], out_sem.at[i])
            store.start()
            stores.append(store)
        for store in stores:
            store.wait()


def ahead(width, shares, deal, six, part):
    cols = six.shape[0]
    any_space = pl.BlockSpec(memory_space=pl.ANY)
    return pl.pallas_call(
        functools.partial(ahead_kernel, width, shares),
        out_shape=jax.ShapeDtypeStruct((cols, cols), jnp.float32),
        in_specs=[any_space] * 3,
        out_specs=any_space,
        scratch_shapes=[
            pltpu.VMEM((cols, cols), jnp.bfloat16),
            pltpu.VMEM(part.shape, jnp.bfloat16),
            pltpu.VMEM((cols, cols), jnp.float32),
            pltpu.SMEM((cols // width,), jnp.int32),
            pltpu.SemaphoreType.DMA,
            pltpu.SemaphoreType.DMA((cols // width,)),
            pltpu.SemaphoreType.DMA,
            pltpu.SemaphoreType.DMA((len(ahead_tiles(cols)),)),
        ],
        cost_estimate=pl.CostEstimate(
            flops=2 * cols**3, bytes_accessed=8 * cols * cols, transcendentals=0
        ),
    )(deal, six, part)


def chain_kernel(width, shares, *refs):
    deal_ref, six_ref = refs[:2]
    part_refs = refs[2 : 2 + shares]
    sum_ref, out_ref, six, part, total, result, deal, deal_sem, six_sem, part_sem, sum_sem, out_sem = (
        refs[2 + shares :]
    )
    cols = six.shape[0]
    step = min(256, cols)
    rows = cols // shares
    was_ahead = lax.rem(lax.axis_index("blk"), 2) == AHEAD

    def form(first):
        if first:
            fetch_sum = pltpu.make_async_copy(sum_ref, total, sum_sem)
            fetch_sum.start()
        parts = [
            pltpu.make_async_copy(part_refs[i], part.at[i], part_sem.at[i])
            for i in range(first, shares)
        ]
        for copy in parts:
            copy.start()
        blocks = fetch_six(width, deal_ref, six_ref, deal, six, deal_sem, six_sem)
        for copy in blocks + parts:
            copy.wait()
        if first:
            fetch_sum.wait()
        stores = []
        for i in range(cols // step):
            at = pl.ds(i * step, step)
            value = total[at, :] if first else None
            for p in range(first, shares):
                value = add_part(six, at, part[p], owner_range(p, shares, rows), value, TERMS)
            result[at, :] = value.astype(jnp.bfloat16)
            store = pltpu.make_async_copy(result.at[at, :], out_ref.at[at, :], out_sem.at[i])
            store.start()
            stores.append(store)
        for store in stores:
            store.wait()

    @pl.when(was_ahead)
    def _():
        form(1)

    @pl.when(jnp.logical_not(was_ahead))
    def _():
        form(0)


def chain(width, deal, six, parts, formed):
    cols = six.shape[0]
    shares = len(parts)
    any_space = pl.BlockSpec(memory_space=pl.ANY)
    return pl.pallas_call(
        functools.partial(chain_kernel, width, shares),
        out_shape=jax.ShapeDtypeStruct((cols, cols), jnp.bfloat16),
        in_specs=[any_space] * (3 + shares),
        out_specs=any_space,
        scratch_shapes=[
            pltpu.VMEM((cols, cols), jnp.bfloat16),
            pltpu.VMEM((shares,) + parts[0].shape, jnp.bfloat16),
            pltpu.VMEM((cols, cols), jnp.float32),
            pltpu.VMEM((cols, cols), jnp.bfloat16),
            pltpu.SMEM((cols // width,), jnp.int32),
            pltpu.SemaphoreType.DMA,
            pltpu.SemaphoreType.DMA((cols // width,)),
            pltpu.SemaphoreType.DMA((shares,)),
            pltpu.SemaphoreType.DMA,
            pltpu.SemaphoreType.DMA((cols // min(256, cols),)),
        ],
        cost_estimate=pl.CostEstimate(
            flops=6 * cols**3, bytes_accessed=6 * cols * cols, transcendentals=0
        ),
    )(deal, six, *parts, formed)


def near_kernel(far_ref, near_ref, sem):
    copy = pltpu.make_async_copy(far_ref, near_ref, sem)
    copy.start()
    copy.wait()


def near(block):
    return pl.pallas_call(
        near_kernel,
        out_shape=jax.ShapeDtypeStruct(block.shape, block.dtype),
        in_specs=[pl.BlockSpec(memory_space=pl.ANY)],
        out_specs=pl.BlockSpec(memory_space=pltpu.VMEM),
        scratch_shapes=[pltpu.SemaphoreType.DMA],
        compiler_params=pltpu.CompilerParams(vmem_limit_bytes=4 * 1024 * 1024),
        cost_estimate=pl.CostEstimate(
            flops=0, bytes_accessed=4 * block.size, transcendentals=0
        ),
    )(block)


def panel_parts(part):
    shares = lax.axis_size("blk")
    parts = [part]
    for _ in range(shares - 1):
        part = lax.ppermute(part, "blk", [(i, (i + 1) % shares) for i in range(shares)])
        parts.append(part)
    return parts


def exchange(block, groups):
    parts = block.reshape(groups, block.shape[0] // groups, block.shape[1])
    parts = lax.all_to_all(
        parts, "chan", split_axis=0, concat_axis=0, tiled=True, axis_index_groups=[ranks(groups)]
    )
    return parts.reshape(block.shape)


def per_device(amps, six_j, interaction, deal, pandya_map, rows_live):
    groups = lax.axis_size("chan")
    _, rows, cols = amps.shape
    width = cols // groups
    parts = panel_parts(interaction[0])
    outgoing = scatter(width, pandya_map, rows_live, amps[0])
    formed = ahead(width, len(parts), deal, six_j[0], parts[0])
    outgoing, formed, *parts = lax.optimization_barrier((outgoing, formed, *parts))
    incoming = exchange(outgoing, groups)
    both = chain(width, deal, six_j[0], parts, formed)
    both = near(both)
    sending = jnp.dot(both, incoming, preferred_element_type=jnp.float32).astype(jnp.bfloat16)
    arriving = exchange(sending, groups)
    result = gather(width, pandya_map, rows_live, arriving)
    return result[None]


def solution(mesh):
    in_specs = (
        P("chan", "blk", None),
        P("chan", None, None),
        P("chan", "blk", None),
        P(),
        P(),
        P(),
    )
    out_specs = P("chan", "blk", None)
    return jax.shard_map(
        per_device, mesh=mesh, in_specs=in_specs, out_specs=out_specs, check_vma=False
    )
```

```python
import functools

import jax
import jax.numpy as jnp
from jax import lax
from jax.experimental import pallas as pl
from jax.experimental.pallas import tpu as pltpu
from jax.sharding import PartitionSpec as P

LANES = 128
AHEAD = 0
RANKS = (9, 13, 8, 6, 10, 2, 14, 11, 12, 1, 0, 3, 15, 5, 4, 7)
TERMS = 3


def ranks(groups):
    return list(RANKS) if groups == len(RANKS) else list(range(groups))


def rank_of(place, groups):
    if groups != len(RANKS):
        return place
    words = [0, 0]
    for rank, at in enumerate(RANKS):
        words[at // 8] |= rank << (at % 8 * 4)
    low, high = (jnp.int32(word - (word >> 31 << 32)) for word in words)
    word = jnp.where(place < 8, low, high)
    return lax.shift_right_logical(word, (place & 7) * 4) & 15


def live_lanes(first, rows, live):
    ids = first + lax.broadcasted_iota(jnp.int32, (LANES, rows), 1)
    return ids < live


def scatter_kernel(
    width, map_ref, live_ref, amps_ref, out_ref, tile, turned, map_in, live_in, sem, out_sem, small
):
    rows, cols = amps_ref.shape
    first = lax.axis_index("blk") * rows
    per_tile = LANES // width
    scalars = [
        pltpu.make_async_copy(map_ref, map_in, small.at[0]),
        pltpu.make_async_copy(live_ref, live_in, small.at[1]),
    ]
    loads = [
        pltpu.make_async_copy(amps_ref.at[:, pl.ds(j * LANES, LANES)], tile.at[j], sem.at[j])
        for j in range(cols // LANES)
    ]
    for copy in scalars + loads:
        copy.start()
    for copy in scalars:
        copy.wait()
    keep = live_lanes(first, rows, live_in[lax.axis_index("chan")])
    stores = []
    for j, load in enumerate(loads):
        load.wait()
        turned[pl.ds(j * LANES, LANES), :] = jnp.where(keep, tile[j].T, 0)
        for k in range(j * per_tile, (j + 1) * per_tile):
            at = pl.multiple_of(rank_of(map_in[k], cols // width) * width, width)
            store = pltpu.make_async_copy(
                turned.at[pl.ds(k * width, width), :],
                out_ref.at[pl.ds(at, width), :],
                out_sem.at[k],
            )
            store.start()
            stores.append(store)
    for store in stores:
        store.wait()


def gather_kernel(width, map_ref, live_ref, back_ref, out_ref, tile, sem):
    rows, cols = out_ref.shape
    first = lax.axis_index("blk") * rows
    live = live_ref[lax.axis_index("chan")]
    per_tile = LANES // width
    keep = live_lanes(first, rows, live)
    stores = []
    for j in range(cols // LANES):
        blocks = []
        for i in range(per_tile):
            rank = rank_of(map_ref[j * per_tile + i], cols // width)
            at = pl.multiple_of(rank * width, width)
            blocks.append(back_ref[pl.ds(at, width), :])
        tile[j] = jnp.where(keep, jnp.concatenate(blocks, axis=0), 0).T
        store = pltpu.make_async_copy(
            tile.at[j], out_ref.at[:, pl.ds(j * LANES, LANES)], sem.at[j]
        )
        store.start()
        stores.append(store)
    for store in stores:
        store.wait()


def scatter(width, pandya_map, rows_live, block):
    rows, cols = block.shape
    count = cols // width
    return pl.pallas_call(
        functools.partial(scatter_kernel, width),
        out_shape=jax.ShapeDtypeStruct((cols, rows), jnp.bfloat16),
        in_specs=[pl.BlockSpec(memory_space=pl.ANY)] * 3,
        out_specs=pl.BlockSpec(memory_space=pl.ANY),
        scratch_shapes=[
            pltpu.VMEM((cols // LANES, rows, LANES), jnp.bfloat16),
            pltpu.VMEM((cols, rows), jnp.bfloat16),
            pltpu.SMEM((count,), jnp.int32),
            pltpu.SMEM((count,), jnp.int32),
            pltpu.SemaphoreType.DMA((cols // LANES,)),
            pltpu.SemaphoreType.DMA((count,)),
            pltpu.SemaphoreType.DMA((2,)),
        ],
        cost_estimate=pl.CostEstimate(
            flops=0, bytes_accessed=4 * cols * rows, transcendentals=0
        ),
    )(pandya_map, rows_live, block)


def gather(width, pandya_map, rows_live, block):
    cols, rows = block.shape
    return pl.pallas_call(
        functools.partial(gather_kernel, width),
        out_shape=jax.ShapeDtypeStruct((rows, cols), jnp.bfloat16),
        in_specs=[
            pl.BlockSpec(memory_space=pltpu.SMEM),
            pl.BlockSpec(memory_space=pltpu.SMEM),
            pl.BlockSpec(memory_space=pltpu.VMEM),
        ],
        out_specs=pl.BlockSpec(memory_space=pl.ANY),
        scratch_shapes=[
            pltpu.VMEM((cols // LANES, rows, LANES), jnp.bfloat16),
            pltpu.SemaphoreType.DMA((cols // LANES,)),
        ],
        compiler_params=pltpu.CompilerParams(vmem_limit_bytes=8 * 1024 * 1024),
        cost_estimate=pl.CostEstimate(
            flops=0, bytes_accessed=4 * cols * rows, transcendentals=0
        ),
    )(pandya_map, rows_live, block)


def add_part(six, at, part, across_at, total, terms):
    across = (((1,), (1,)), ((), ()))
    rest = lax.dot_general(six[at, :], part, across, preferred_element_type=jnp.float32)
    for _ in range(terms):
        term = rest.astype(jnp.bfloat16)
        rest = rest - term.astype(jnp.float32)
        share = lax.dot_general(
            term, six[:, across_at], across, preferred_element_type=jnp.float32
        )
        total = share if total is None else total + share
    return total


def fetch_six(width, deal_ref, six_ref, deal, six, deal_sem, six_sem):
    fetch_deal = pltpu.make_async_copy(deal_ref, deal, deal_sem)
    fetch_deal.start()
    fetch_deal.wait()
    blocks = [
        pltpu.make_async_copy(
            six_ref.at[pl.ds(pl.multiple_of(deal[s] * width, width), width), :],
            six.at[pl.ds(r * width, width), :],
            six_sem.at[r],
        )
        for r, s in enumerate(ranks(six.shape[0] // width))
    ]
    for copy in blocks:
        copy.start()
    return blocks


def owner_range(i, shares, rows):
    owner = lax.rem(lax.axis_index("blk") + shares - i, shares)
    return pl.ds(pl.multiple_of(owner * rows, rows), rows)


def ahead_tiles(cols):
    step = min(256, cols)
    starts = [0, step // 2] + list(range(step, cols, step))
    return [(a, b - a) for a, b in zip(starts, starts[1:] + [cols])]


def ahead_kernel(
    width, shares, deal_ref, six_ref, part_ref, sum_ref, six, part, total, deal, deal_sem, six_sem, part_sem, out_sem
):
    cols = six.shape[0]
    tiles = ahead_tiles(cols)

    @pl.when(lax.rem(lax.axis_index("blk"), 2) == AHEAD)
    def _():
        fetch_part = pltpu.make_async_copy(part_ref, part, part_sem)
        fetch_part.start()
        for copy in fetch_six(width, deal_ref, six_ref, deal, six, deal_sem, six_sem):
            copy.wait()
        fetch_part.wait()
        stores = []
        for i, (start, size) in enumerate(tiles):
            at = pl.ds(start, size)
            total[at, :] = add_part(
                six, at, part[...], owner_range(0, shares, part.shape[0]), None, TERMS
            )
            store = pltpu.make_async_copy(total.at[at, :], sum_ref.at[at, :], out_sem.at[i])
            store.start()
            stores.append(store)
        for store in stores:
            store.wait()


def ahead(width, shares, deal, six, part):
    cols = six.shape[0]
    any_space = pl.BlockSpec(memory_space=pl.ANY)
    return pl.pallas_call(
        functools.partial(ahead_kernel, width, shares),
        out_shape=jax.ShapeDtypeStruct((cols, cols), jnp.float32),
        in_specs=[any_space] * 3,
        out_specs=any_space,
        scratch_shapes=[
            pltpu.VMEM((cols, cols), jnp.bfloat16),
            pltpu.VMEM(part.shape, jnp.bfloat16),
            pltpu.VMEM((cols, cols), jnp.float32),
            pltpu.SMEM((cols // width,), jnp.int32),
            pltpu.SemaphoreType.DMA,
            pltpu.SemaphoreType.DMA((cols // width,)),
            pltpu.SemaphoreType.DMA,
            pltpu.SemaphoreType.DMA((len(ahead_tiles(cols)),)),
        ],
        cost_estimate=pl.CostEstimate(
            flops=2 * cols**3, bytes_accessed=8 * cols * cols, transcendentals=0
        ),
    )(deal, six, part)


def chain_kernel(width, shares, *refs):
    deal_ref, six_ref = refs[:2]
    part_refs = refs[2 : 2 + shares]
    sum_ref, out_ref, six, part, total, result, deal, deal_sem, six_sem, part_sem, sum_sem, out_sem = (
        refs[2 + shares :]
    )
    cols = six.shape[0]
    step = min(256, cols)
    rows = cols // shares
    was_ahead = lax.rem(lax.axis_index("blk"), 2) == AHEAD

    def form(first):
        if first:
            fetch_sum = pltpu.make_async_copy(sum_ref, total, sum_sem)
            fetch_sum.start()
        parts = [
            pltpu.make_async_copy(part_refs[i], part.at[i], part_sem.at[i])
            for i in range(first, shares)
        ]
        for copy in parts:
            copy.start()
        blocks = fetch_six(width, deal_ref, six_ref, deal, six, deal_sem, six_sem)
        for copy in blocks + parts:
            copy.wait()
        if first:
            fetch_sum.wait()
        stores = []
        for i in range(cols // step):
            at = pl.ds(i * step, step)
            value = total[at, :] if first else None
            for p in range(first, shares):
                value = add_part(six, at, part[p], owner_range(p, shares, rows), value, TERMS)
            result[at, :] = value.astype(jnp.bfloat16)
            store = pltpu.make_async_copy(result.at[at, :], out_ref.at[at, :], out_sem.at[i])
            store.start()
            stores.append(store)
        for store in stores:
            store.wait()

    @pl.when(was_ahead)
    def _():
        form(1)

    @pl.when(jnp.logical_not(was_ahead))
    def _():
        form(0)


def chain(width, deal, six, parts, formed):
    cols = six.shape[0]
    shares = len(parts)
    any_space = pl.BlockSpec(memory_space=pl.ANY)
    return pl.pallas_call(
        functools.partial(chain_kernel, width, shares),
        out_shape=jax.ShapeDtypeStruct((cols, cols), jnp.bfloat16),
        in_specs=[any_space] * (3 + shares),
        out_specs=any_space,
        scratch_shapes=[
            pltpu.VMEM((cols, cols), jnp.bfloat16),
            pltpu.VMEM((shares,) + parts[0].shape, jnp.bfloat16),
            pltpu.VMEM((cols, cols), jnp.float32),
            pltpu.VMEM((cols, cols), jnp.bfloat16),
            pltpu.SMEM((cols // width,), jnp.int32),
            pltpu.SemaphoreType.DMA,
            pltpu.SemaphoreType.DMA((cols // width,)),
            pltpu.SemaphoreType.DMA((shares,)),
            pltpu.SemaphoreType.DMA,
            pltpu.SemaphoreType.DMA((cols // min(256, cols),)),
        ],
        cost_estimate=pl.CostEstimate(
            flops=6 * cols**3, bytes_accessed=6 * cols * cols, transcendentals=0
        ),
    )(deal, six, *parts, formed)


def near_kernel(far_ref, near_ref, sem):
    copy = pltpu.make_async_copy(far_ref, near_ref, sem)
    copy.start()
    copy.wait()


def near(block):
    return pl.pallas_call(
        near_kernel,
        out_shape=jax.ShapeDtypeStruct(block.shape, block.dtype),
        in_specs=[pl.BlockSpec(memory_space=pl.ANY)],
        out_specs=pl.BlockSpec(memory_space=pltpu.VMEM),
        scratch_shapes=[pltpu.SemaphoreType.DMA],
        compiler_params=pltpu.CompilerParams(vmem_limit_bytes=4 * 1024 * 1024),
        cost_estimate=pl.CostEstimate(
            flops=0, bytes_accessed=4 * block.size, transcendentals=0
        ),
    )(block)


def panel_parts(part):
    shares = lax.axis_size("blk")
    parts = [part]
    for _ in range(shares - 1):
        part = lax.ppermute(part, "blk", [(i, (i + 1) % shares) for i in range(shares)])
        parts.append(part)
    return parts


def exchange(block, groups):
    parts = block.reshape(groups, block.shape[0] // groups, block.shape[1])
    parts = lax.all_to_all(
        parts, "chan", split_axis=0, concat_axis=0, tiled=True, axis_index_groups=[ranks(groups)]
    )
    return parts.reshape(block.shape)


def per_device(amps, six_j, interaction, deal, pandya_map, rows_live):
    groups = lax.axis_size("chan")
    _, rows, cols = amps.shape
    width = cols // groups
    parts = panel_parts(interaction[0])
    outgoing = scatter(width, pandya_map, rows_live, amps[0])
    formed = ahead(width, len(parts), deal, six_j[0], parts[0])
    outgoing, formed, *parts = lax.optimization_barrier((outgoing, formed, *parts))
    incoming = exchange(outgoing, groups)
    both = chain(width, deal, six_j[0], parts, formed)
    both = near(both)
    sending = jnp.dot(both, incoming, preferred_element_type=jnp.float32).astype(jnp.bfloat16)
    arriving = exchange(sending, groups)
    result = gather(width, pandya_map, rows_live, arriving)
    return result[None]


def solution(mesh):
    in_specs = (
        P("chan", "blk", None),
        P("chan", None, None),
        P("chan", "blk", None),
        P(),
        P(),
        P(),
    )
    out_specs = P("chan", "blk", None)
    return jax.shard_map(
        per_device, mesh=mesh, in_specs=in_specs, out_specs=out_specs, check_vma=False
    )
```

```python
import functools

import jax
import jax.numpy as jnp
from jax import lax
from jax.experimental import pallas as pl
from jax.experimental.pallas import tpu as pltpu
from jax.sharding import PartitionSpec as P

LANES = 128
AHEAD = 0
RANKS = (8, 13, 4, 0, 12, 10, 14, 9, 2, 6, 5, 1, 3, 11, 7, 15)
TERMS = 3


def ranks(groups):
    return list(RANKS) if groups == len(RANKS) else list(range(groups))


def rank_of(place, groups):
    if groups != len(RANKS):
        return place
    words = [0, 0]
    for rank, at in enumerate(RANKS):
        words[at // 8] |= rank << (at % 8 * 4)
    low, high = (jnp.int32(word - (word >> 31 << 32)) for word in words)
    word = jnp.where(place < 8, low, high)
    return lax.shift_right_logical(word, (place & 7) * 4) & 15


def live_lanes(first, rows, live):
    ids = first + lax.broadcasted_iota(jnp.int32, (LANES, rows), 1)
    return ids < live


def scatter_kernel(
    width, map_ref, live_ref, amps_ref, out_ref, tile, turned, map_in, live_in, sem, out_sem, small
):
    rows, cols = amps_ref.shape
    first = lax.axis_index("blk") * rows
    per_tile = LANES // width
    scalars = [
        pltpu.make_async_copy(map_ref, map_in, small.at[0]),
        pltpu.make_async_copy(live_ref, live_in, small.at[1]),
    ]
    loads = [
        pltpu.make_async_copy(amps_ref.at[:, pl.ds(j * LANES, LANES)], tile.at[j], sem.at[j])
        for j in range(cols // LANES)
    ]
    for copy in scalars + loads:
        copy.start()
    for copy in scalars:
        copy.wait()
    keep = live_lanes(first, rows, live_in[lax.axis_index("chan")])
    stores = []
    for j, load in enumerate(loads):
        load.wait()
        turned[pl.ds(j * LANES, LANES), :] = jnp.where(keep, tile[j].T, 0)
        for k in range(j * per_tile, (j + 1) * per_tile):
            at = pl.multiple_of(rank_of(map_in[k], cols // width) * width, width)
            store = pltpu.make_async_copy(
                turned.at[pl.ds(k * width, width), :],
                out_ref.at[pl.ds(at, width), :],
                out_sem.at[k],
            )
            store.start()
            stores.append(store)
    for store in stores:
        store.wait()


def gather_kernel(width, map_ref, live_ref, back_ref, out_ref, tile, sem):
    rows, cols = out_ref.shape
    first = lax.axis_index("blk") * rows
    live = live_ref[lax.axis_index("chan")]
    per_tile = LANES // width
    keep = live_lanes(first, rows, live)
    stores = []
    for j in range(cols // LANES):
        blocks = []
        for i in range(per_tile):
            rank = rank_of(map_ref[j * per_tile + i], cols // width)
            at = pl.multiple_of(rank * width, width)
            blocks.append(back_ref[pl.ds(at, width), :])
        tile[j] = jnp.where(keep, jnp.concatenate(blocks, axis=0), 0).T
        store = pltpu.make_async_copy(
            tile.at[j], out_ref.at[:, pl.ds(j * LANES, LANES)], sem.at[j]
        )
        store.start()
        stores.append(store)
    for store in stores:
        store.wait()


def scatter(width, pandya_map, rows_live, block):
    rows, cols = block.shape
    count = cols // width
    return pl.pallas_call(
        functools.partial(scatter_kernel, width),
        out_shape=jax.ShapeDtypeStruct((cols, rows), jnp.bfloat16),
        in_specs=[pl.BlockSpec(memory_space=pl.ANY)] * 3,
        out_specs=pl.BlockSpec(memory_space=pl.ANY),
        scratch_shapes=[
            pltpu.VMEM((cols // LANES, rows, LANES), jnp.bfloat16),
            pltpu.VMEM((cols, rows), jnp.bfloat16),
            pltpu.SMEM((count,), jnp.int32),
            pltpu.SMEM((count,), jnp.int32),
            pltpu.SemaphoreType.DMA((cols // LANES,)),
            pltpu.SemaphoreType.DMA((count,)),
            pltpu.SemaphoreType.DMA((2,)),
        ],
        cost_estimate=pl.CostEstimate(
            flops=0, bytes_accessed=4 * cols * rows, transcendentals=0
        ),
    )(pandya_map, rows_live, block)


def gather(width, pandya_map, rows_live, block):
    cols, rows = block.shape
    return pl.pallas_call(
        functools.partial(gather_kernel, width),
        out_shape=jax.ShapeDtypeStruct((rows, cols), jnp.bfloat16),
        in_specs=[
            pl.BlockSpec(memory_space=pltpu.SMEM),
            pl.BlockSpec(memory_space=pltpu.SMEM),
            pl.BlockSpec(memory_space=pltpu.VMEM),
        ],
        out_specs=pl.BlockSpec(memory_space=pl.ANY),
        scratch_shapes=[
            pltpu.VMEM((cols // LANES, rows, LANES), jnp.bfloat16),
            pltpu.SemaphoreType.DMA((cols // LANES,)),
        ],
        compiler_params=pltpu.CompilerParams(vmem_limit_bytes=8 * 1024 * 1024),
        cost_estimate=pl.CostEstimate(
            flops=0, bytes_accessed=4 * cols * rows, transcendentals=0
        ),
    )(pandya_map, rows_live, block)


def add_part(six, at, part, across_at, total, terms):
    across = (((1,), (1,)), ((), ()))
    rest = lax.dot_general(six[at, :], part, across, preferred_element_type=jnp.float32)
    for _ in range(terms):
        term = rest.astype(jnp.bfloat16)
        rest = rest - term.astype(jnp.float32)
        share = lax.dot_general(
            term, six[:, across_at], across, preferred_element_type=jnp.float32
        )
        total = share if total is None else total + share
    return total


def fetch_six(width, deal_ref, six_ref, deal, six, deal_sem, six_sem):
    fetch_deal = pltpu.make_async_copy(deal_ref, deal, deal_sem)
    fetch_deal.start()
    fetch_deal.wait()
    blocks = [
        pltpu.make_async_copy(
            six_ref.at[pl.ds(pl.multiple_of(deal[s] * width, width), width), :],
            six.at[pl.ds(r * width, width), :],
            six_sem.at[r],
        )
        for r, s in enumerate(ranks(six.shape[0] // width))
    ]
    for copy in blocks:
        copy.start()
    return blocks


def owner_range(i, shares, rows):
    owner = lax.rem(lax.axis_index("blk") + shares - i, shares)
    return pl.ds(pl.multiple_of(owner * rows, rows), rows)


def ahead_tiles(cols):
    step = min(256, cols)
    starts = [0, step // 2] + list(range(step, cols, step))
    return [(a, b - a) for a, b in zip(starts, starts[1:] + [cols])]


def ahead_kernel(
    width, shares, deal_ref, six_ref, part_ref, sum_ref, six, part, total, deal, deal_sem, six_sem, part_sem, out_sem
):
    cols = six.shape[0]
    tiles = ahead_tiles(cols)

    @pl.when(lax.rem(lax.axis_index("blk"), 2) == AHEAD)
    def _():
        fetch_part = pltpu.make_async_copy(part_ref, part, part_sem)
        fetch_part.start()
        for copy in fetch_six(width, deal_ref, six_ref, deal, six, deal_sem, six_sem):
            copy.wait()
        fetch_part.wait()
        stores = []
        for i, (start, size) in enumerate(tiles):
            at = pl.ds(start, size)
            total[at, :] = add_part(
                six, at, part[...], owner_range(0, shares, part.shape[0]), None, TERMS
            )
            store = pltpu.make_async_copy(total.at[at, :], sum_ref.at[at, :], out_sem.at[i])
            store.start()
            stores.append(store)
        for store in stores:
            store.wait()


def ahead(width, shares, deal, six, part):
    cols = six.shape[0]
    any_space = pl.BlockSpec(memory_space=pl.ANY)
    return pl.pallas_call(
        functools.partial(ahead_kernel, width, shares),
        out_shape=jax.ShapeDtypeStruct((cols, cols), jnp.float32),
        in_specs=[any_space] * 3,
        out_specs=any_space,
        scratch_shapes=[
            pltpu.VMEM((cols, cols), jnp.bfloat16),
            pltpu.VMEM(part.shape, jnp.bfloat16),
            pltpu.VMEM((cols, cols), jnp.float32),
            pltpu.SMEM((cols // width,), jnp.int32),
            pltpu.SemaphoreType.DMA,
            pltpu.SemaphoreType.DMA((cols // width,)),
            pltpu.SemaphoreType.DMA,
            pltpu.SemaphoreType.DMA((len(ahead_tiles(cols)),)),
        ],
        cost_estimate=pl.CostEstimate(
            flops=2 * cols**3, bytes_accessed=8 * cols * cols, transcendentals=0
        ),
    )(deal, six, part)


def chain_kernel(width, shares, *refs):
    deal_ref, six_ref = refs[:2]
    part_refs = refs[2 : 2 + shares]
    sum_ref, out_ref, six, part, total, result, deal, deal_sem, six_sem, part_sem, sum_sem, out_sem = (
        refs[2 + shares :]
    )
    cols = six.shape[0]
    step = min(256, cols)
    rows = cols // shares
    was_ahead = lax.rem(lax.axis_index("blk"), 2) == AHEAD

    def form(first):
        if first:
            fetch_sum = pltpu.make_async_copy(sum_ref, total, sum_sem)
            fetch_sum.start()
        parts = [
            pltpu.make_async_copy(part_refs[i], part.at[i], part_sem.at[i])
            for i in range(first, shares)
        ]
        for copy in parts:
            copy.start()
        blocks = fetch_six(width, deal_ref, six_ref, deal, six, deal_sem, six_sem)
        for copy in blocks + parts:
            copy.wait()
        if first:
            fetch_sum.wait()
        stores = []
        for i in range(cols // step):
            at = pl.ds(i * step, step)
            value = total[at, :] if first else None
            for p in range(first, shares):
                value = add_part(six, at, part[p], owner_range(p, shares, rows), value, TERMS)
            result[at, :] = value.astype(jnp.bfloat16)
            store = pltpu.make_async_copy(result.at[at, :], out_ref.at[at, :], out_sem.at[i])
            store.start()
            stores.append(store)
        for store in stores:
            store.wait()

    @pl.when(was_ahead)
    def _():
        form(1)

    @pl.when(jnp.logical_not(was_ahead))
    def _():
        form(0)


def chain(width, deal, six, parts, formed):
    cols = six.shape[0]
    shares = len(parts)
    any_space = pl.BlockSpec(memory_space=pl.ANY)
    return pl.pallas_call(
        functools.partial(chain_kernel, width, shares),
        out_shape=jax.ShapeDtypeStruct((cols, cols), jnp.bfloat16),
        in_specs=[any_space] * (3 + shares),
        out_specs=any_space,
        scratch_shapes=[
            pltpu.VMEM((cols, cols), jnp.bfloat16),
            pltpu.VMEM((shares,) + parts[0].shape, jnp.bfloat16),
            pltpu.VMEM((cols, cols), jnp.float32),
            pltpu.VMEM((cols, cols), jnp.bfloat16),
            pltpu.SMEM((cols // width,), jnp.int32),
            pltpu.SemaphoreType.DMA,
            pltpu.SemaphoreType.DMA((cols // width,)),
            pltpu.SemaphoreType.DMA((shares,)),
            pltpu.SemaphoreType.DMA,
            pltpu.SemaphoreType.DMA((cols // min(256, cols),)),
        ],
        cost_estimate=pl.CostEstimate(
            flops=6 * cols**3, bytes_accessed=6 * cols * cols, transcendentals=0
        ),
    )(deal, six, *parts, formed)


def near_kernel(far_ref, near_ref, sem):
    copy = pltpu.make_async_copy(far_ref, near_ref, sem)
    copy.start()
    copy.wait()


def near(block):
    return pl.pallas_call(
        near_kernel,
        out_shape=jax.ShapeDtypeStruct(block.shape, block.dtype),
        in_specs=[pl.BlockSpec(memory_space=pl.ANY)],
        out_specs=pl.BlockSpec(memory_space=pltpu.VMEM),
        scratch_shapes=[pltpu.SemaphoreType.DMA],
        compiler_params=pltpu.CompilerParams(vmem_limit_bytes=4 * 1024 * 1024),
        cost_estimate=pl.CostEstimate(
            flops=0, bytes_accessed=4 * block.size, transcendentals=0
        ),
    )(block)


def panel_parts(part):
    shares = lax.axis_size("blk")
    parts = [part]
    for _ in range(shares - 1):
        part = lax.ppermute(part, "blk", [(i, (i + 1) % shares) for i in range(shares)])
        parts.append(part)
    return parts


def exchange(block, groups):
    parts = block.reshape(groups, block.shape[0] // groups, block.shape[1])
    parts = lax.all_to_all(
        parts, "chan", split_axis=0, concat_axis=0, tiled=True, axis_index_groups=[ranks(groups)]
    )
    return parts.reshape(block.shape)


def per_device(amps, six_j, interaction, deal, pandya_map, rows_live):
    groups = lax.axis_size("chan")
    _, rows, cols = amps.shape
    width = cols // groups
    parts = panel_parts(interaction[0])
    outgoing = scatter(width, pandya_map, rows_live, amps[0])
    formed = ahead(width, len(parts), deal, six_j[0], parts[0])
    outgoing, formed, *parts = lax.optimization_barrier((outgoing, formed, *parts))
    incoming = exchange(outgoing, groups)
    both = chain(width, deal, six_j[0], parts, formed)
    both = near(both)
    sending = jnp.dot(both, incoming, preferred_element_type=jnp.float32).astype(jnp.bfloat16)
    arriving = exchange(sending, groups)
    result = gather(width, pandya_map, rows_live, arriving)
    return result[None]


def solution(mesh):
    in_specs = (
        P("chan", "blk", None),
        P("chan", None, None),
        P("chan", "blk", None),
        P(),
        P(),
        P(),
    )
    out_specs = P("chan", "blk", None)
    return jax.shard_map(
        per_device, mesh=mesh, in_specs=in_specs, out_specs=out_specs, check_vma=False
    )
```

```python
import functools

import jax
import jax.numpy as jnp
from jax import lax
from jax.experimental import pallas as pl
from jax.experimental.pallas import tpu as pltpu
from jax.sharding import PartitionSpec as P

LANES = 128
AHEAD = 0
RANKS = (8, 13, 4, 0, 12, 10, 14, 9, 2, 6, 5, 1, 3, 11, 7, 15)
TERMS = 3


def ranks(groups):
    return list(RANKS) if groups == len(RANKS) else list(range(groups))


def rank_of(place, groups):
    if groups != len(RANKS):
        return place
    words = [0, 0]
    for rank, at in enumerate(RANKS):
        words[at // 8] |= rank << (at % 8 * 4)
    low, high = (jnp.int32(word - (word >> 31 << 32)) for word in words)
    word = jnp.where(place < 8, low, high)
    return lax.shift_right_logical(word, (place & 7) * 4) & 15


def live_lanes(first, rows, live):
    ids = first + lax.broadcasted_iota(jnp.int32, (LANES, rows), 1)
    return ids < live


def scatter_kernel(
    width, map_ref, live_ref, amps_ref, out_ref, tile, turned, map_in, live_in, sem, out_sem, small
):
    rows, cols = amps_ref.shape
    first = lax.axis_index("blk") * rows
    per_tile = LANES // width
    scalars = [
        pltpu.make_async_copy(map_ref, map_in, small.at[0]),
        pltpu.make_async_copy(live_ref, live_in, small.at[1]),
    ]
    loads = [
        pltpu.make_async_copy(amps_ref.at[:, pl.ds(j * LANES, LANES)], tile.at[j], sem.at[j])
        for j in range(cols // LANES)
    ]
    for copy in scalars + loads:
        copy.start()
    for copy in scalars:
        copy.wait()
    keep = live_lanes(first, rows, live_in[lax.axis_index("chan")])
    stores = []
    for j, load in enumerate(loads):
        load.wait()
        turned[pl.ds(j * LANES, LANES), :] = jnp.where(keep, tile[j].T, 0)
        for k in range(j * per_tile, (j + 1) * per_tile):
            at = pl.multiple_of(rank_of(map_in[k], cols // width) * width, width)
            store = pltpu.make_async_copy(
                turned.at[pl.ds(k * width, width), :],
                out_ref.at[pl.ds(at, width), :],
                out_sem.at[k],
            )
            store.start()
            stores.append(store)
    for store in stores:
        store.wait()


def gather_kernel(width, map_ref, live_ref, back_ref, out_ref, tile, sem):
    rows, cols = out_ref.shape
    first = lax.axis_index("blk") * rows
    live = live_ref[lax.axis_index("chan")]
    per_tile = LANES // width
    keep = live_lanes(first, rows, live)
    stores = []
    for j in range(cols // LANES):
        blocks = []
        for i in range(per_tile):
            rank = rank_of(map_ref[j * per_tile + i], cols // width)
            at = pl.multiple_of(rank * width, width)
            blocks.append(back_ref[pl.ds(at, width), :])
        tile[:, pl.ds(j * LANES, LANES)] = jnp.where(keep, jnp.concatenate(blocks, axis=0), 0).T
        if j % 2:
            at = pl.ds((j - 1) * LANES, 2 * LANES)
            store = pltpu.make_async_copy(tile.at[:, at], out_ref.at[:, at], sem.at[j // 2])
            store.start()
            stores.append(store)
    for store in stores:
        store.wait()


def scatter(width, pandya_map, rows_live, block):
    rows, cols = block.shape
    count = cols // width
    return pl.pallas_call(
        functools.partial(scatter_kernel, width),
        out_shape=jax.ShapeDtypeStruct((cols, rows), jnp.bfloat16),
        in_specs=[pl.BlockSpec(memory_space=pl.ANY)] * 3,
        out_specs=pl.BlockSpec(memory_space=pl.ANY),
        scratch_shapes=[
            pltpu.VMEM((cols // LANES, rows, LANES), jnp.bfloat16),
            pltpu.VMEM((cols, rows), jnp.bfloat16),
            pltpu.SMEM((count,), jnp.int32),
            pltpu.SMEM((count,), jnp.int32),
            pltpu.SemaphoreType.DMA((cols // LANES,)),
            pltpu.SemaphoreType.DMA((count,)),
            pltpu.SemaphoreType.DMA((2,)),
        ],
        cost_estimate=pl.CostEstimate(
            flops=0, bytes_accessed=4 * cols * rows, transcendentals=0
        ),
    )(pandya_map, rows_live, block)


def gather(width, pandya_map, rows_live, block):
    cols, rows = block.shape
    return pl.pallas_call(
        functools.partial(gather_kernel, width),
        out_shape=jax.ShapeDtypeStruct((rows, cols), jnp.bfloat16),
        in_specs=[
            pl.BlockSpec(memory_space=pltpu.SMEM),
            pl.BlockSpec(memory_space=pltpu.SMEM),
            pl.BlockSpec(memory_space=pltpu.VMEM),
        ],
        out_specs=pl.BlockSpec(memory_space=pl.ANY),
        scratch_shapes=[
            pltpu.VMEM((rows, cols), jnp.bfloat16),
            pltpu.SemaphoreType.DMA((cols // LANES,)),
        ],
        compiler_params=pltpu.CompilerParams(vmem_limit_bytes=8 * 1024 * 1024),
        cost_estimate=pl.CostEstimate(
            flops=0, bytes_accessed=4 * cols * rows, transcendentals=0
        ),
    )(pandya_map, rows_live, block)


def add_part(six, at, part, across_at, total, terms):
    across = (((1,), (1,)), ((), ()))
    rest = lax.dot_general(six[at, :], part, across, preferred_element_type=jnp.float32)
    for _ in range(terms):
        term = rest.astype(jnp.bfloat16)
        rest = rest - term.astype(jnp.float32)
        share = lax.dot_general(
            term, six[:, across_at], across, preferred_element_type=jnp.float32
        )
        total = share if total is None else total + share
    return total


def fetch_six(width, deal_ref, six_ref, deal, six, deal_sem, six_sem):
    fetch_deal = pltpu.make_async_copy(deal_ref, deal, deal_sem)
    fetch_deal.start()
    fetch_deal.wait()
    blocks = [
        pltpu.make_async_copy(
            six_ref.at[pl.ds(pl.multiple_of(deal[s] * width, width), width), :],
            six.at[pl.ds(r * width, width), :],
            six_sem.at[r],
        )
        for r, s in enumerate(ranks(six.shape[0] // width))
    ]
    for copy in blocks:
        copy.start()
    return blocks


def owner_range(i, shares, rows):
    owner = lax.rem(lax.axis_index("blk") + shares - i, shares)
    return pl.ds(pl.multiple_of(owner * rows, rows), rows)


def ahead_tiles(cols):
    step = min(256, cols)
    starts = [0, step // 2] + list(range(step, cols, step))
    return [(a, b - a) for a, b in zip(starts, starts[1:] + [cols])]


def ahead_kernel(
    width, shares, deal_ref, six_ref, part_ref, sum_ref, six, part, total, deal, deal_sem, six_sem, part_sem, out_sem
):
    cols = six.shape[0]
    tiles = ahead_tiles(cols)

    @pl.when(lax.rem(lax.axis_index("blk"), 2) == AHEAD)
    def _():
        fetch_part = pltpu.make_async_copy(part_ref, part, part_sem)
        fetch_part.start()
        for copy in fetch_six(width, deal_ref, six_ref, deal, six, deal_sem, six_sem):
            copy.wait()
        fetch_part.wait()
        stores = []
        for i, (start, size) in enumerate(tiles):
            at = pl.ds(start, size)
            total[at, :] = add_part(
                six, at, part[...], owner_range(0, shares, part.shape[0]), None, TERMS
            )
            store = pltpu.make_async_copy(total.at[at, :], sum_ref.at[at, :], out_sem.at[i])
            store.start()
            stores.append(store)
        for store in stores:
            store.wait()


def ahead(width, shares, deal, six, part):
    cols = six.shape[0]
    any_space = pl.BlockSpec(memory_space=pl.ANY)
    return pl.pallas_call(
        functools.partial(ahead_kernel, width, shares),
        out_shape=jax.ShapeDtypeStruct((cols, cols), jnp.float32),
        in_specs=[any_space] * 3,
        out_specs=any_space,
        scratch_shapes=[
            pltpu.VMEM((cols, cols), jnp.bfloat16),
            pltpu.VMEM(part.shape, jnp.bfloat16),
            pltpu.VMEM((cols, cols), jnp.float32),
            pltpu.SMEM((cols // width,), jnp.int32),
            pltpu.SemaphoreType.DMA,
            pltpu.SemaphoreType.DMA((cols // width,)),
            pltpu.SemaphoreType.DMA,
            pltpu.SemaphoreType.DMA((len(ahead_tiles(cols)),)),
        ],
        cost_estimate=pl.CostEstimate(
            flops=2 * cols**3, bytes_accessed=8 * cols * cols, transcendentals=0
        ),
    )(deal, six, part)


def chain_kernel(width, shares, *refs):
    deal_ref, six_ref = refs[:2]
    part_refs = refs[2 : 2 + shares]
    sum_ref, out_ref, six, part, total, result, deal, deal_sem, six_sem, part_sem, sum_sem, out_sem = (
        refs[2 + shares :]
    )
    cols = six.shape[0]
    step = min(256, cols)
    rows = cols // shares
    was_ahead = lax.rem(lax.axis_index("blk"), 2) == AHEAD

    def form(first):
        if first:
            fetch_sum = pltpu.make_async_copy(sum_ref, total, sum_sem)
            fetch_sum.start()
        parts = [
            pltpu.make_async_copy(part_refs[i], part.at[i], part_sem.at[i])
            for i in range(first, shares)
        ]
        for copy in parts:
            copy.start()
        blocks = fetch_six(width, deal_ref, six_ref, deal, six, deal_sem, six_sem)
        for copy in blocks + parts:
            copy.wait()
        if first:
            fetch_sum.wait()
        stores = []
        for i in range(cols // step):
            at = pl.ds(i * step, step)
            value = total[at, :] if first else None
            for p in range(first, shares):
                value = add_part(six, at, part[p], owner_range(p, shares, rows), value, TERMS)
            result[at, :] = value.astype(jnp.bfloat16)
            store = pltpu.make_async_copy(result.at[at, :], out_ref.at[at, :], out_sem.at[i])
            store.start()
            stores.append(store)
        for store in stores:
            store.wait()

    @pl.when(was_ahead)
    def _():
        form(1)

    @pl.when(jnp.logical_not(was_ahead))
    def _():
        form(0)


def chain(width, deal, six, parts, formed):
    cols = six.shape[0]
    shares = len(parts)
    any_space = pl.BlockSpec(memory_space=pl.ANY)
    return pl.pallas_call(
        functools.partial(chain_kernel, width, shares),
        out_shape=jax.ShapeDtypeStruct((cols, cols), jnp.bfloat16),
        in_specs=[any_space] * (3 + shares),
        out_specs=any_space,
        scratch_shapes=[
            pltpu.VMEM((cols, cols), jnp.bfloat16),
            pltpu.VMEM((shares,) + parts[0].shape, jnp.bfloat16),
            pltpu.VMEM((cols, cols), jnp.float32),
            pltpu.VMEM((cols, cols), jnp.bfloat16),
            pltpu.SMEM((cols // width,), jnp.int32),
            pltpu.SemaphoreType.DMA,
            pltpu.SemaphoreType.DMA((cols // width,)),
            pltpu.SemaphoreType.DMA((shares,)),
            pltpu.SemaphoreType.DMA,
            pltpu.SemaphoreType.DMA((cols // min(256, cols),)),
        ],
        cost_estimate=pl.CostEstimate(
            flops=6 * cols**3, bytes_accessed=6 * cols * cols, transcendentals=0
        ),
    )(deal, six, *parts, formed)


def near_kernel(far_ref, near_ref, sem):
    copy = pltpu.make_async_copy(far_ref, near_ref, sem)
    copy.start()
    copy.wait()


def near(block):
    return pl.pallas_call(
        near_kernel,
        out_shape=jax.ShapeDtypeStruct(block.shape, block.dtype),
        in_specs=[pl.BlockSpec(memory_space=pl.ANY)],
        out_specs=pl.BlockSpec(memory_space=pltpu.VMEM),
        scratch_shapes=[pltpu.SemaphoreType.DMA],
        compiler_params=pltpu.CompilerParams(vmem_limit_bytes=4 * 1024 * 1024),
        cost_estimate=pl.CostEstimate(
            flops=0, bytes_accessed=4 * block.size, transcendentals=0
        ),
    )(block)


def panel_parts(part):
    shares = lax.axis_size("blk")
    parts = [part]
    for _ in range(shares - 1):
        part = lax.ppermute(part, "blk", [(i, (i + 1) % shares) for i in range(shares)])
        parts.append(part)
    return parts


def exchange(block, groups):
    parts = block.reshape(groups, block.shape[0] // groups, block.shape[1])
    parts = lax.all_to_all(
        parts, "chan", split_axis=0, concat_axis=0, tiled=True, axis_index_groups=[ranks(groups)]
    )
    return parts.reshape(block.shape)


def per_device(amps, six_j, interaction, deal, pandya_map, rows_live):
    groups = lax.axis_size("chan")
    _, rows, cols = amps.shape
    width = cols // groups
    parts = panel_parts(interaction[0])
    outgoing = scatter(width, pandya_map, rows_live, amps[0])
    formed = ahead(width, len(parts), deal, six_j[0], parts[0])
    outgoing, formed, *parts = lax.optimization_barrier((outgoing, formed, *parts))
    incoming = exchange(outgoing, groups)
    both = chain(width, deal, six_j[0], parts, formed)
    both = near(both)
    sending = jnp.dot(both, incoming, preferred_element_type=jnp.float32).astype(jnp.bfloat16)
    arriving = exchange(sending, groups)
    result = gather(width, pandya_map, rows_live, arriving)
    return result[None]


def solution(mesh):
    in_specs = (
        P("chan", "blk", None),
        P("chan", None, None),
        P("chan", "blk", None),
        P(),
        P(),
        P(),
    )
    out_specs = P("chan", "blk", None)
    return jax.shard_map(
        per_device, mesh=mesh, in_specs=in_specs, out_specs=out_specs, check_vma=False
    )
```
